32 devices in a mesh: col: 4 (over x, core), row: 8 (over z, y).
Axes of the slice: x: 2, y: 2, z: 4, core: 2. Of those that a mesh axis runs over, the one named last changes fastest.
Arguments:
- features: float32 [4096, 512], P(('row', 'col')), may hold values from -6 to 6
- weight: float32 [512, 512], replicated, may hold values from -0.25 to 0.25
- tiles: bfloat16 [4, 8, 6, 128, 128], P('col', 'row'), may hold values from -0.1875 to 0.1875
- tile_rows: int32 [4, 8, 6], P('col', 'row'), may hold values from 0 to 7, as said below
- tile_cols: int32 [4, 8, 6], P('col', 'row'), may hold values from 0 to 3
- tile_count: int32 [4, 8], P('col', 'row'), may hold values from 1 to 6, as said below
- cotangent: bfloat16 [4096, 512], P(('col', 'row')), may hold values from -6 to 6
Outputs:
- aggregated: bfloat16 [4096, 512], P(('col', 'row'))
- grad_x: float32 [4096, 512], P(('row', 'col'))
- grad_w: float32 [512, 512], replicated
The draws below stay inside these ranges and needn't reach their ends.
Inputs may be any that keep to these rules, and one draw needn't show every extreme that they name: `tile_rows`: within one grid block the live slots name distinct tiles. `tile_count`: some grid block has all 6 slots live.
All inputs are finite; a program needn't handle non-finite values.
Results may differ from the reference program's by a relative error of at most 0.0049.
Values may be sent and summed in bfloat16 or wider, within the bound.
A program may use at most 128 MiB of HBM per device.

```python
import jax
import jax.numpy as jnp
from jax import lax

F = 512
TILE = 128
ROWS_DEV = 128
NODES = 4096
MAXT = 6
N_COL = 4
N_ROW = 8


def tile_layout(key):
    dst_tiles = ROWS_DEV * N_ROW // TILE
    src_tiles = ROWS_DEV * N_COL // TILE
    keys = jax.random.split(jax.random.fold_in(key, 7), N_COL * N_ROW)
    chosen = jax.vmap(lambda one_key: jax.random.permutation(one_key, dst_tiles * src_tiles)[:MAXT])(keys)
    return (chosen.reshape(N_COL, N_ROW, MAXT).astype(jnp.int32), src_tiles)


def draw_tile_rows(key, part):
    chosen, src_tiles = tile_layout(key)
    return (chosen // src_tiles).astype(jnp.int32)


def draw_tile_cols(key, part):
    chosen, src_tiles = tile_layout(key)
    return (chosen % src_tiles).astype(jnp.int32)


def draw_tile_count(key, part):
    first_key = jax.random.fold_in(key, 11)
    second_key = jax.random.fold_in(key, 13)
    raw_draw = jax.random.randint(first_key, (N_COL * N_ROW,), 0, MAXT + 1)
    counts = 1 + raw_draw * raw_draw // (MAXT + 1)
    position = jax.random.randint(second_key, (), 0, N_COL * N_ROW)
    counts = counts.at[position].set(MAXT)
    return counts.reshape(N_COL, N_ROW).astype(jnp.int32)


def steps_of(key, shape, shards, smallest, high):
    level, own = 1.0, jax.random.fold_in(key, 6)
    for axis_at, parts in shards:
        steps = jnp.exp(jax.random.uniform(jax.random.fold_in(own, axis_at), (parts,), jnp.float32, smallest / len(shards), high / len(shards)))
        level = level * jnp.repeat(steps, shape[axis_at] // parts).reshape([-1 if axis == axis_at else 1 for axis in range(len(shape))])
    return level


def centred(rng, shape, deviation, most, pieces=(), kind=jnp.bfloat16):
    loudness = steps_of(rng, shape, pieces, -0.22, 0.18) if pieces else 1.0
    array = jax.random.normal(rng, shape, jnp.float32) * deviation * loudness
    return jnp.minimum(jnp.maximum(array, -most), most).astype(kind)


def setup_inputs(seed: int = 0) -> dict:
    streams_of = jax.random.split(jax.random.key(seed), 8)
    features = centred(streams_of[0], (NODES, F), 1.0, 6.0, ((0, 32),), jnp.float32)
    weight = centred(streams_of[1], (F, F), F ** -0.5, 0.25, (), jnp.float32)
    tiles = centred(streams_of[2], (N_COL, N_ROW, MAXT, TILE, TILE), (ROWS_DEV * N_ROW) ** -0.5, 0.1875, ((0, 4), (1, 8)))
    tile_rows = draw_tile_rows(jax.random.fold_in(streams_of[7], 71), 0)
    tile_cols = draw_tile_cols(jax.random.fold_in(streams_of[7], 71), 0)
    tile_count = draw_tile_count(jax.random.fold_in(streams_of[7], 71), 0)
    cotangent = centred(streams_of[6], (NODES, F), 1.0, 6.0, ((0, 32),))
    return dict(features=features, weight=weight, tiles=tiles, tile_rows=tile_rows, tile_cols=tile_cols, tile_count=tile_count, cotangent=cotangent)


def reference(features, weight, tiles, tile_rows, tile_cols, tile_count, cotangent):
    dst_tiles = ROWS_DEV * N_ROW // TILE
    src_tiles = ROWS_DEV * N_COL // TILE
    projected = jnp.dot(features, weight, precision=lax.Precision.HIGHEST, preferred_element_type=jnp.float32).astype(jnp.bfloat16)
    projected = projected.reshape(N_ROW, src_tiles, TILE, F)
    grads = cotangent.reshape(N_COL, dst_tiles, TILE, F)
    slot_ids = jnp.arange(MAXT, dtype=jnp.int32)

    def step(carry, index):
        agg_sum, back_sum = carry
        col_id = index // N_ROW
        row_id = index % N_ROW
        blocks = tiles[col_id, row_id]
        rows_idx = tile_rows[col_id, row_id]
        cols_idx = tile_cols[col_id, row_id]
        live_slots = slot_ids < tile_count[col_id, row_id]
        picked = projected[row_id][cols_idx]
        tile_terms = jnp.einsum("tab,tbf->taf", blocks.astype(jnp.float32), picked.astype(jnp.float32))
        select_dst = ((rows_idx[None, :] == jnp.arange(dst_tiles, dtype=jnp.int32)[:, None]) & live_slots[None, :]).astype(jnp.float32)
        agg_sum = agg_sum.at[col_id].add(jnp.einsum("it,taf->iaf", select_dst, tile_terms, precision=lax.Precision.HIGHEST))
        picked_g = grads[col_id][rows_idx]
        back_terms = jnp.einsum("tab,taf->tbf", blocks.astype(jnp.float32), picked_g.astype(jnp.float32))
        select_src = ((cols_idx[None, :] == jnp.arange(src_tiles, dtype=jnp.int32)[:, None]) & live_slots[None, :]).astype(jnp.float32)
        back_sum = back_sum.at[row_id].add(jnp.einsum("kt,tbf->kbf", select_src, back_terms, precision=lax.Precision.HIGHEST))
        return (agg_sum, back_sum), None

    start = (jnp.zeros((N_COL, dst_tiles, TILE, F), jnp.float32), jnp.zeros((N_ROW, src_tiles, TILE, F), jnp.float32))
    (agg_sum, back_sum), _ = lax.scan(step, start, jnp.arange(N_COL * N_ROW, dtype=jnp.int32))
    aggregated = agg_sum.reshape(NODES, F).astype(jnp.bfloat16)
    grad_y = back_sum.reshape(NODES, F)
    grad_x = jnp.dot(grad_y, weight.T, precision=lax.Precision.HIGHEST, preferred_element_type=jnp.float32)
    grad_w = jnp.dot(features.T, grad_y, precision=lax.Precision.HIGHEST, preferred_element_type=jnp.float32)
    return (aggregated, grad_x, grad_w)
```

```python
import functools

import jax
import jax.numpy as jnp
from jax import lax
from jax.experimental import pallas as pl
from jax.experimental.pallas import tpu as pltpu
from jax.sharding import PartitionSpec as P

BF16 = jnp.bfloat16
F32 = jnp.float32
MESH = pl.DeviceIdType.MESH


def each(count, body):
    if count <= 8:
        for step in range(count):
            body(step)
    else:
        lax.fori_loop(0, count, lambda step, _: (body(step), None)[1], None)


def matmul(a, b, contract=((1,), (0,))):
    return lax.dot_general(a, b, (contract, ((), ())), preferred_element_type=F32)


def layer_kernel(
    n_col, n_row, inner, pieces,
    rows_ref, cols_ref, count_ref, feat_ref, w_ref, tiles_ref, cot_ref,
    agg_ref, gx_ref, gw_ref,
    feat_all, cot_all, pad, pad_t, a_ref, at_ref, w_hi, w_lo, proj, part, part_send, y_in, z_in,
    back, back_send, c_in, g_part, g1_in, g1_sum, g2_in, gw_all,
    feat_s, feat_r, cotz_s, coty_s, cot_r, py_s, py_r, pz_s, pz_r, c_s, c_r,
    g1_s, g1_r, g2_s, g2_r, g3_s, g3_r, g4_s, g4_r,
):
    outer = n_row // inner
    slots, tile = tiles_ref.shape[0], tiles_ref.shape[1]
    rows_dev, width = cot_ref.shape
    per_dev = rows_dev // tile
    dst_tiles, src_tiles = n_row * per_dev, n_col * per_dev
    col, row = lax.axis_index("col"), lax.axis_index("row")
    out_id, in_id = row // inner, row % inner
    g_rows = width // n_col
    g_piece = g_rows // pieces

    def send(src, dst, s_sem, r_sem, target):
        copy = pltpu.make_async_remote_copy(
            src_ref=src, dst_ref=dst, send_sem=s_sem, recv_sem=r_sem,
            device_id=target, device_id_type=MESH,
        )
        copy.start()

    def sent(ref, s_sem):
        pltpu.make_async_remote_copy(
            src_ref=ref, dst_ref=ref, send_sem=s_sem, recv_sem=s_sem,
            device_id={"col": col}, device_id_type=MESH,
        ).wait_send()

    def landed(ref, r_sem):
        pltpu.make_async_remote_copy(
            src_ref=ref, dst_ref=ref, send_sem=r_sem, recv_sem=r_sem,
            device_id={"col": col}, device_id_type=MESH,
        ).wait_recv()

    def col_at(d):
        return lax.rem(col + d, n_col)

    def row_at(d):
        return lax.rem(row + d, n_row)

    def out_at(d):
        return lax.rem(out_id + d, outer)

    def in_at(d):
        return lax.rem(in_id + d, inner)

    def reducer(r, body):
        if pieces == n_row:
            body()
        else:
            pl.when(r < pieces)(body)

    barrier = pltpu.get_barrier_semaphore()
    each(n_col - 1, lambda d: pl.semaphore_signal(
        barrier, inc=1, device_id={"col": col_at(d + 1)}, device_id_type=MESH))
    each(n_row - 1, lambda d: pl.semaphore_signal(
        barrier, inc=1, device_id={"row": row_at(d + 1)}, device_id_type=MESH))
    feat_all[col] = feat_ref[...].astype(BF16)
    cot_all[row] = cot_ref[...]
    pl.semaphore_wait(barrier, n_col + n_row - 2)

    def cot_out(d):
        send(cot_ref, cot_all.at[row], cotz_s.at[d], cot_r.at[row], {"row": out_at(d + 1) * inner + in_id})

    def cot_forward(o, d_out):
        def one(d):
            slot = o * inner + in_id
            send(cot_all.at[slot], cot_all.at[slot], coty_s.at[d_out, d], cot_r.at[slot],
                 {"row": out_id * inner + in_at(d + 1)})
        each(inner - 1, one)

    each(outer - 1, cot_out)
    cot_forward(out_id, 0)

    def feat_out(d):
        send(feat_all.at[col], feat_all.at[col], feat_s.at[d], feat_r.at[col], {"col": col_at(d + 1)})

    each(n_col - 1, feat_out)

    def pad_one(t):
        one = tiles_ref[t]
        pad[t] = one
        pad_t[t] = one.T

    each(slots, pad_one)
    pad[slots] = jnp.zeros((tile, tile), BF16)
    pad_t[slots] = jnp.zeros((tile, tile), BF16)
    live = count_ref[0]
    places = [
        jnp.where(t < live, rows_ref[t] * src_tiles + cols_ref[t], -1) for t in range(slots)
    ]

    def lay(i):
        for k in range(src_tiles):
            index = jnp.int32(slots)
            for t in range(slots):
                index = jnp.where(places[t] == i * src_tiles + k, t, index)
            at = i * tile if isinstance(i, int) else pl.multiple_of(i * tile, tile)
            a_ref[pl.ds(at, tile), k * tile:(k + 1) * tile] = pad[index]
            at_ref[k * tile:(k + 1) * tile, pl.ds(at, tile)] = pad_t[index]

    each(dst_tiles, lay)
    weight = w_ref[...]
    w_hi[...] = weight.astype(BF16)
    w_lo[...] = (weight - w_hi[...].astype(F32)).astype(BF16)

    def project(d):
        c = col_at(d)
        if not (isinstance(d, int) and d == 0):
            landed(feat_all.at[c], feat_r.at[c])
        block = feat_all[c]
        proj[pl.ds(pl.multiple_of(c * rows_dev, rows_dev), rows_dev), :] = (
            matmul(block, w_hi[...]) + matmul(block, w_lo[...])
        ).astype(BF16)

    project(0)
    each(n_col - 1, lambda d: project(d + 1))

    def pass_on(d):
        o = out_at(d + 1)
        landed(cot_all.at[o * inner + in_id], cot_r.at[o * inner + in_id])
        cot_forward(o, d + 1)

    each(outer - 1, pass_on)

    def forward(d):
        o = out_at(d + 1)
        span = inner * rows_dev
        block = a_ref[pl.ds(pl.multiple_of(o * span, span), span), :]
        result = matmul(block, proj[...]).reshape(inner, rows_dev, width)
        part[o] = result
        part_send[o] = result.astype(BF16)

        def one(e):
            target = in_at(e + 1)
            send(part_send.at[o, target], y_in.at[o, in_id], py_s.at[o, e], py_r.at[o, in_id],
                 {"row": out_id * inner + target})
        each(inner - 1, one)

    each(outer, forward)

    def backward(d):
        o = out_at(d)
        span = inner * rows_dev

        def one(e):
            slot = o * inner + in_at(e + 1)
            landed(cot_all.at[slot], cot_r.at[slot])
        each(inner - 1, one)
        block = at_ref[:, pl.ds(pl.multiple_of(o * span, span), span)]
        cots = cot_all[pl.ds(o * inner, inner)].reshape(span, width)
        term = matmul(block, cots)
        if isinstance(d, int) and d == 0:
            back[...] = term
        else:
            back[...] += term

    backward(0)
    each(outer - 1, lambda d: backward(d + 1))
    back_send[...] = back[...].astype(BF16).reshape(n_col, rows_dev, width)

    g_part[...] = matmul(
        feat_all[...].reshape(n_col * rows_dev, width),
        back_send[...].reshape(n_col * rows_dev, width),
        ((0,), (0,)),
    ).astype(BF16).reshape(n_col, g_rows, width)

    def g1_out(d):
        c = col_at(d + 1)
        send(g_part.at[c], g1_in.at[col], g1_s.at[d], g1_r.at[col], {"col": c})

    def c_out(d):
        c = col_at(d + 1)
        send(back_send.at[c], c_in.at[col], c_s.at[d], c_r.at[col], {"col": c})

    each(n_col - 1, g1_out)
    each(n_col - 1, c_out)

    def inner_sum(o):
        def one(e):
            source = in_at(e + 1)
            landed(y_in.at[o, source], py_r.at[o, source])
            part[o, in_id] += y_in[o, source].astype(F32)
        each(inner - 1, one)

    def outer_out(d):
        o = out_at(d + 1)
        inner_sum(o)
        part_send[o, in_id] = part[o, in_id].astype(BF16)
        send(part_send.at[o, in_id], z_in.at[out_id], pz_s.at[d], pz_r.at[out_id], {"row": o * inner + in_id})

    each(outer - 1, outer_out)
    inner_sum(out_id)

    gw_part = g_part[col].astype(F32)
    def g1_add(d, total):
        c = col_at(d + 1)
        landed(g1_in.at[c], g1_r.at[c])
        return total + g1_in[c].astype(F32)
    for d in range(n_col - 1):
        gw_part = g1_add(d, gw_part)
    g1_sum[...] = gw_part.astype(BF16).reshape(pieces, g_piece, width)

    def g2_out(d):
        r = row_at(d + 1)
        reducer(r, lambda: send(g1_sum.at[r], g2_in.at[row], g2_s.at[d], g2_r.at[row], {"row": r}))

    each(n_row - 1, g2_out)

    def c_add(d):
        c = col_at(d + 1)
        landed(c_in.at[c], c_r.at[c])
    each(n_col - 1, c_add)
    grad_y = back[pl.ds(pl.multiple_of(col * rows_dev, rows_dev), rows_dev), :]
    for d in range(n_col - 1):
        grad_y = grad_y + c_in[col_at(d + 1)].astype(F32)
    grad_y = grad_y.astype(BF16)
    gx_ref[...] = matmul(grad_y, w_hi[...], ((1,), (1,))) + matmul(grad_y, w_lo[...], ((1,), (1,)))

    def g2_sum():
        def g2_wait(d):
            r = row_at(d + 1)
            landed(g2_in.at[r], g2_r.at[r])
        each(n_row - 1, g2_wait)
        g2_in[row] = g1_sum[row]
        total = g2_in[0].astype(F32)
        for r in range(1, n_row):
            total = total + g2_in[r].astype(F32)
        gw_all[col, row] = total.astype(BF16)

        def g3_out(d):
            send(gw_all.at[col, row], gw_all.at[col, row], g3_s.at[d], g3_r.at[row], {"row": row_at(d + 1)})
        each(n_row - 1, g3_out)

    reducer(row, g2_sum)

    def z_wait(d):
        o = out_at(d + 1)
        landed(z_in.at[o], pz_r.at[o])
        part[out_id, in_id] += z_in[o].astype(F32)

    each(outer - 1, z_wait)
    agg_ref[...] = part[out_id, in_id].astype(BF16)

    def g3_wait(d):
        r = row_at(d + 1)
        reducer(r, lambda: landed(gw_all.at[col, r], g3_r.at[r]))

    each(n_row - 1, g3_wait)

    def g4_out(d):
        send(gw_all.at[col], gw_all.at[col], g4_s.at[d], g4_r.at[col], {"col": col_at(d + 1)})

    each(n_col - 1, g4_out)

    def g4_wait(d):
        c = col_at(d + 1)
        landed(gw_all.at[c], g4_r.at[c])
        gw_ref[pl.ds(pl.multiple_of(c * g_rows, g_rows), g_rows), :] = (
            gw_all[c].reshape(g_rows, width).astype(F32))

    gw_ref[pl.ds(pl.multiple_of(col * g_rows, g_rows), g_rows), :] = (
        gw_all[col].reshape(g_rows, width).astype(F32))
    each(n_col - 1, g4_wait)

    each(n_col - 1, lambda d: sent(feat_all.at[0], feat_s.at[d]))
    each(outer - 1, lambda d: sent(cot_ref, cotz_s.at[d]))
    each(outer, lambda d: each(inner - 1, lambda e: sent(cot_ref, coty_s.at[d, e])))
    each(outer, lambda d: each(inner - 1, lambda e: sent(y_in.at[0, 0], py_s.at[d, e])))
    each(outer - 1, lambda d: sent(z_in.at[0], pz_s.at[d]))
    each(n_col - 1, lambda d: sent(c_in.at[0], c_s.at[d]))
    each(n_col - 1, lambda d: sent(g1_in.at[0], g1_s.at[d]))
    each(n_row - 1, lambda d: reducer(row_at(d + 1), lambda: sent(g2_in.at[0], g2_s.at[d])))
    reducer(row, lambda: each(n_row - 1, lambda d: sent(g2_in.at[0], g3_s.at[d])))
    each(n_col - 1, lambda d: sent(gw_all.at[0], g4_s.at[d]))


def shards(n_col, n_row, features, weight, tiles, tile_rows, tile_cols, tile_count, cotangent):
    slots, tile = tiles.shape[2], tiles.shape[-1]
    rows_dev, width = features.shape
    inner = 2 if n_row % 2 == 0 else 1
    outer = n_row // inner
    g_rows = width // n_col
    pieces = min(n_row, g_rows // 16)
    g_piece = g_rows // pieces
    src, dst = n_col * rows_dev, n_row * rows_dev
    dma = pltpu.SemaphoreType.DMA
    vmem = pl.BlockSpec(memory_space=pltpu.VMEM)
    smem = pl.BlockSpec(memory_space=pltpu.SMEM)
    buffers = [
        ((n_col, rows_dev, width), BF16),
        ((n_row, rows_dev, width), BF16),
        ((slots + 1, tile, tile), BF16),
        ((slots + 1, tile, tile), BF16),
        ((dst, src), BF16),
        ((src, dst), BF16),
        ((width, width), BF16),
        ((width, width), BF16),
        ((src, width), BF16),
        ((outer, inner, rows_dev, width), F32),
        ((outer, inner, rows_dev, width), BF16),
        ((outer, inner, rows_dev, width), BF16),
        ((outer, rows_dev, width), BF16),
        ((src, width), F32),
        ((n_col, rows_dev, width), BF16),
        ((n_col, rows_dev, width), BF16),
        ((n_col, g_rows, width), BF16),
        ((n_col, g_rows, width), BF16),
        ((pieces, g_piece, width), BF16),
        ((n_row, g_piece, width), BF16),
        ((n_col, pieces, g_piece, width), BF16),
    ]
    sems = [
        (n_col,), (n_col,), (outer,), (outer, inner), (n_row,), (outer, inner), (outer, inner),
        (outer,), (outer,), (n_col,), (n_col,), (n_col,), (n_col,), (n_row,), (n_row,),
        (n_row,), (n_row,), (n_col,), (n_col,),
    ]
    return pl.pallas_call(
        functools.partial(layer_kernel, n_col, n_row, inner, pieces),
        out_shape=(
            jax.ShapeDtypeStruct((rows_dev, width), BF16),
            jax.ShapeDtypeStruct((rows_dev, width), F32),
            jax.ShapeDtypeStruct((width, width), F32),
        ),
        in_specs=[smem] * 3 + [vmem] * 4,
        out_specs=(vmem, vmem, vmem),
        scratch_shapes=[pltpu.VMEM(shape, kind) for shape, kind in buffers] + [dma(s) for s in sems],
        compiler_params=pltpu.CompilerParams(
            collective_id=0, has_side_effects=True, vmem_limit_bytes=56 * 2**20
        ),
        name="layer",
    )(
        tile_rows.reshape(slots), tile_cols.reshape(slots), tile_count.reshape(1),
        features, weight, tiles[0, 0], cotangent,
    )


def solution(mesh):
    placed = (
        P(("row", "col"), None),
        P(),
        P("col", "row", None, None, None),
        P("col", "row", None),
        P("col", "row", None),
        P("col", "row"),
        P(("col", "row"), None),
    )
    return jax.shard_map(
        functools.partial(shards, mesh.shape["col"], mesh.shape["row"]),
        mesh=mesh,
        in_specs=placed,
        out_specs=(P(("col", "row"), None), P(("row", "col"), None), P()),
        check_vma=False,
    )
```

```python
import functools
import math

import jax
import jax.numpy as jnp
from jax import lax
from jax.experimental import pallas as pl
from jax.experimental.pallas import tpu as pltpu
from jax.sharding import PartitionSpec as P

BF16 = jnp.bfloat16
F32 = jnp.float32
MESH = pl.DeviceIdType.MESH


def each(count, body):
    if count <= 8:
        for step in range(count):
            body(step)
    else:
        lax.fori_loop(0, count, lambda step, _: (body(step), None)[1], None)


def matmul(a, b, contract=((1,), (0,))):
    return lax.dot_general(a, b, (contract, ((), ())), preferred_element_type=F32)


def layer_kernel(
    n_col, n_row, inner, near, pieces,
    rows_ref, cols_ref, count_ref, feat_ref, w_ref, tiles_ref, cot_ref,
    agg_ref, gx_ref, gw_ref,
    feat_all, feat_t, ax_t, cot_all, pad, pad_t, a_ref, at_ref, w_hi, w_lo, proj, part, part_send, y_in, z_in,
    back, back_send, c_in, g_sum, g_part, g1_in, g1_sum, g2_in, gw_all,
    feat_s, feat_r, up_s, down_s, coty_s, cot_r, py_s, py_r, pz_s, pz_r, c_s, c_r,
    g1_s, g1_r, g2_s, g2_r, g3_s, g3_r, g4_s, g4_r, g5_s,
):
    outer = n_row // inner
    slots, tile = tiles_ref.shape[0], tiles_ref.shape[1]
    rows_dev, width = cot_ref.shape
    per_dev = rows_dev // tile
    dst_tiles, src_tiles = n_row * per_dev, n_col * per_dev
    col, row = lax.axis_index("col"), lax.axis_index("row")
    out_id, in_id = row // inner, row % inner
    g_rows = width // n_col
    g_piece = g_rows // pieces

    def send(src, dst, s_sem, r_sem, target):
        copy = pltpu.make_async_remote_copy(
            src_ref=src, dst_ref=dst, send_sem=s_sem, recv_sem=r_sem,
            device_id=target, device_id_type=MESH,
        )
        copy.start()

    def sent(ref, s_sem):
        pltpu.make_async_remote_copy(
            src_ref=ref, dst_ref=ref, send_sem=s_sem, recv_sem=s_sem,
            device_id={"col": col}, device_id_type=MESH,
        ).wait_send()

    def landed(ref, r_sem):
        pltpu.make_async_remote_copy(
            src_ref=ref, dst_ref=ref, send_sem=r_sem, recv_sem=r_sem,
            device_id={"col": col}, device_id_type=MESH,
        ).wait_recv()

    def col_at(d):
        return lax.rem(col + d, n_col)

    def row_at(d):
        return lax.rem(row + d, n_row)

    def out_at(d):
        return lax.rem(out_id + d, outer)

    def in_at(d):
        return lax.rem(in_id + d, inner)

    def reducer(r, body):
        if pieces == n_row:
            body()
        else:
            pl.when(r < pieces)(body)

    barrier = pltpu.get_barrier_semaphore()
    each(n_col - 1, lambda d: pl.semaphore_signal(
        barrier, inc=1, device_id={"col": col_at(d + 1)}, device_id_type=MESH))
    each(n_row - 1, lambda d: pl.semaphore_signal(
        barrier, inc=1, device_id={"row": row_at(d + 1)}, device_id_type=MESH))
    feat_all[col] = feat_ref[...].astype(BF16)
    cot_all[row] = cot_ref[...]
    pl.semaphore_wait(barrier, n_col + n_row - 2)

    def chain(o, step, sems, d):
        slot = o * inner + in_id
        to = out_id + step
        send(cot_all.at[slot], cot_all.at[slot], sems.at[d], cot_r.at[slot], {"row": to * inner + in_id})

    def cot_forward(o, d_out):
        def one(d):
            slot = o * inner + in_id
            send(cot_all.at[slot], cot_all.at[slot], coty_s.at[d_out, d], cot_r.at[slot],
                 {"row": out_id * inner + in_at(d + 1)})
        each(inner - 1, one)

    if outer > 1:
        pl.when(out_id < outer - 1)(lambda: chain(out_id, 1, up_s, 0))
        pl.when(out_id > 0)(lambda: chain(out_id, -1, down_s, 0))
    cot_forward(out_id, 0)

    def feat_out(d):
        send(feat_all.at[col], feat_all.at[col], feat_s.at[d], feat_r.at[col], {"col": col_at(d + 1)})

    each(n_col - 1, feat_out)

    def pad_one(t):
        one = tiles_ref[t]
        pad[t] = one
        pad_t[t] = one.T

    each(slots, pad_one)
    pad[slots] = jnp.zeros((tile, tile), BF16)
    pad_t[slots] = jnp.zeros((tile, tile), BF16)
    live = count_ref[0]
    places = [
        jnp.where(t < live, rows_ref[t] * src_tiles + cols_ref[t], -1) for t in range(slots)
    ]

    def lay(i):
        for k in range(src_tiles):
            index = jnp.int32(slots)
            for t in range(slots):
                index = jnp.where(places[t] == i * src_tiles + k, t, index)
            at = i * tile if isinstance(i, int) else pl.multiple_of(i * tile, tile)
            a_ref[pl.ds(at, tile), k * tile:(k + 1) * tile] = pad[index]
            at_ref[k * tile:(k + 1) * tile, pl.ds(at, tile)] = pad_t[index]

    each(dst_tiles, lay)
    weight = w_ref[...]
    w_hi[...] = weight.astype(BF16)
    w_lo[...] = (weight - w_hi[...].astype(F32)).astype(BF16)

    def project(d):
        c = col_at(d)
        if not (isinstance(d, int) and d == 0):
            landed(feat_all.at[c], feat_r.at[c])
        block = feat_all[c]
        at = pl.multiple_of(c * rows_dev, rows_dev)
        proj[pl.ds(at, rows_dev), :] = (
            matmul(block, w_hi[...]) + matmul(block, w_lo[...])
        ).astype(BF16)
        feat_t[:, pl.ds(at, rows_dev)] = block.T

    project(0)

    def pass_on(d):
        def from_below():
            o = out_id - d
            landed(cot_all.at[o * inner + in_id], cot_r.at[o * inner + in_id])
            pl.when(out_id < outer - 1)(lambda: chain(o, 1, up_s, d))
            cot_forward(o, o + 1)

        def from_above():
            o = out_id + d
            landed(cot_all.at[o * inner + in_id], cot_r.at[o * inner + in_id])
            pl.when(out_id > 0)(lambda: chain(o, -1, down_s, d))
            cot_forward(o, o + 1)

        pl.when(out_id - d >= 0)(from_below)
        pl.when(out_id + d < outer)(from_above)

    span = inner * rows_dev

    def forward(o):
        at = o * span if isinstance(o, int) else pl.multiple_of(o * span, span)
        result = matmul(a_ref[pl.ds(at, span), :], proj[...]).reshape(inner, rows_dev, width)
        part[o] = result
        part_send[o] = result.astype(BF16)

    def weight_term(d):
        def add(o):
            def one(e):
                slot = o * inner + in_at(e + 1)
                landed(cot_all.at[slot], cot_r.at[slot])
            each(inner - 1, one)
            block = ax_t[:, pl.ds(pl.multiple_of(o * span, span), span)]
            g_sum[...] += matmul(block, cot_all[pl.ds(o * inner, inner)].reshape(span, width))

        if isinstance(d, int) and d == 0:
            add(out_id)
        else:
            pl.when(out_id - d >= 0)(lambda: add(out_id - d))
            pl.when(out_id + d < outer)(lambda: add(out_id + d))

    each(n_col - 1, lambda d: project(d + 1))
    if outer > 1:
        pass_on(1)
    ax_t[...] = matmul(feat_t[...], at_ref[...]).astype(BF16)
    g_sum[...] = jnp.zeros_like(g_sum)
    each(outer - 2, lambda d: pass_on(d + 2))
    each(outer, forward)
    weight_term(0)
    each(outer - 1, lambda d: weight_term(d + 1))
    g_part[...] = g_sum[...].astype(BF16).reshape(n_col, g_rows, width)

    def g1_out(d):
        c = col_at(d + 1)
        send(g_part.at[c], g1_in.at[col], g1_s.at[d], g1_r.at[col], {"col": c})

    each(n_col - 1, g1_out)

    def inner_out(d):
        o = out_at(d + 1)

        def one(e):
            target = in_at(e + 1)
            send(part_send.at[o, target], y_in.at[o, in_id], py_s.at[o, e], py_r.at[o, in_id],
                 {"row": out_id * inner + target})
        each(inner - 1, one)

    each(outer, inner_out)

    back[...] = matmul(at_ref[...], cot_all[...].reshape(n_row * rows_dev, width))
    back_send[...] = back[...].astype(BF16).reshape(n_col, rows_dev, width)

    def c_out(d):
        c = col_at(d + 1)
        send(back_send.at[c], c_in.at[col], c_s.at[d], c_r.at[col], {"col": c})

    gw_part = g_part[col].astype(F32)
    def g1_add(d, total):
        c = col_at(d + 1)
        landed(g1_in.at[c], g1_r.at[c])
        return total + g1_in[c].astype(F32)
    for d in range(n_col - 1):
        gw_part = g1_add(d, gw_part)
    g1_sum[...] = gw_part.astype(BF16).reshape(pieces, g_piece, width)

    def g2_out(d):
        r = row_at(d + 1)
        reducer(r, lambda: send(g1_sum.at[r], g2_in.at[row], g2_s.at[d], g2_r.at[row], {"row": r}))

    each(n_row - 1, g2_out)
    each(n_col - 1, c_out)

    def inner_sum(o):
        def one(e):
            source = in_at(e + 1)
            landed(y_in.at[o, source], py_r.at[o, source])
            part[o, in_id] += y_in[o, source].astype(F32)
        each(inner - 1, one)

    def outer_out(d):
        o = out_at(d + 1)
        inner_sum(o)
        part_send[o, in_id] = part[o, in_id].astype(BF16)
        send(part_send.at[o, in_id], z_in.at[out_id], pz_s.at[d], pz_r.at[out_id], {"row": o * inner + in_id})

    each(outer - 1, outer_out)
    inner_sum(out_id)

    def g2_sum():
        def g2_wait(d):
            r = row_at(d + 1)
            landed(g2_in.at[r], g2_r.at[r])
        each(n_row - 1, g2_wait)
        g2_in[row] = g1_sum[row]
        total = g2_in[0].astype(F32)
        for r in range(1, n_row):
            total = total + g2_in[r].astype(F32)
        gw_all[col, row] = total.astype(BF16)

        def g3_out(d):
            send(gw_all.at[col, row], gw_all.at[col, row], g3_s.at[d], g3_r.at[row], {"row": row_at(d + 1)})
        each(n_row - 1, g3_out)

    reducer(row, g2_sum)

    def c_add(d):
        c = col_at(d + 1)
        landed(c_in.at[c], c_r.at[c])
    each(n_col - 1, c_add)
    grad_y = back[pl.ds(pl.multiple_of(col * rows_dev, rows_dev), rows_dev), :]
    for d in range(n_col - 1):
        grad_y = grad_y + c_in[col_at(d + 1)].astype(F32)
    grad_y = grad_y.astype(BF16)
    gx_ref[...] = matmul(grad_y, w_hi[...], ((1,), (1,))) + matmul(grad_y, w_lo[...], ((1,), (1,)))

    def z_wait(d):
        o = out_at(d + 1)
        landed(z_in.at[o], pz_r.at[o])
        part[out_id, in_id] += z_in[o].astype(F32)

    each(outer - 1, z_wait)
    agg_ref[...] = part[out_id, in_id].astype(BF16)

    def outer_col(d):
        return lax.rem(col // near + d, n_col // near) * near + col % near

    def near_col(d):
        return col // near * near + lax.rem(col % near + d, near)

    def to_near(c, r, d):
        def one(e):
            send(gw_all.at[c, r], gw_all.at[c, r], g5_s.at[d, r, e], g4_r.at[c, r], {"col": near_col(e + 1)})
        each(near - 1, one)

    def piece_out(r):
        def one(d):
            send(gw_all.at[col, r], gw_all.at[col, r], g4_s.at[d, r], g4_r.at[col, r], {"col": outer_col(d + 1)})
        each(n_col // near - 1, one)
        to_near(col, r, 0)

    def g3_wait(d):
        r = row_at(d + 1)

        def piece():
            landed(gw_all.at[col, r], g3_r.at[r])
            piece_out(r)
        reducer(r, piece)

    reducer(row, lambda: piece_out(row))
    each(n_row - 1, g3_wait)

    def pass_piece(d):
        c = outer_col(d + 1)

        def one(e):
            r = row_at(e)

            def piece():
                landed(gw_all.at[c, r], g4_r.at[c, r])
                to_near(c, r, d + 1)
            reducer(r, piece)
        each(n_row, one)

    each(n_col // near - 1, pass_piece)

    def last_wait(d):
        def one(e):
            c = near_col(e + 1)
            c = lax.rem(c // near + d, n_col // near) * near + c % near
            each(pieces, lambda r: landed(gw_all.at[c, r], g4_r.at[c, r]))
        each(near - 1, one)

    each(n_col // near, last_wait)
    gw_ref[...] = gw_all[...].reshape(width, width)

    each(n_col - 1, lambda d: sent(feat_all.at[0], feat_s.at[d]))
    def chain_sent(d):
        def up():
            sent(cot_ref, up_s.at[d])

        def down():
            sent(cot_ref, down_s.at[d])
        pl.when((out_id - d >= 0) & (out_id < outer - 1))(up)
        pl.when((out_id + d < outer) & (out_id > 0))(down)

    if outer > 1:
        each(outer, chain_sent)
    each(outer, lambda o: each(inner - 1, lambda e: sent(
        cot_ref, coty_s.at[jnp.where(out_id == o, 0, o + 1), e])))
    each(outer, lambda d: each(inner - 1, lambda e: sent(y_in.at[0, 0], py_s.at[d, e])))
    each(outer - 1, lambda d: sent(z_in.at[0], pz_s.at[d]))
    each(n_col - 1, lambda d: sent(c_in.at[0], c_s.at[d]))
    each(n_col - 1, lambda d: sent(g1_in.at[0], g1_s.at[d]))
    each(n_row - 1, lambda d: reducer(row_at(d + 1), lambda: sent(g2_in.at[0], g2_s.at[d])))
    reducer(row, lambda: each(n_row - 1, lambda d: sent(g2_in.at[0], g3_s.at[d])))
    each(pieces, lambda r: each(n_col // near - 1, lambda d: sent(g2_in.at[0], g4_s.at[d, r])))
    each(pieces, lambda r: each(n_col // near, lambda d: each(
        near - 1, lambda e: sent(g2_in.at[0], g5_s.at[d, r, e]))))


def write_kernel(agg_ref, gx_ref, gw_ref, agg_out, gx_out, gw_out):
    agg_out[...] = agg_ref[...]
    gx_out[...] = gx_ref[...]
    gw_out[...] = gw_ref[...].astype(F32)


def shards(n_col, n_row, features, weight, tiles, tile_rows, tile_cols, tile_count, cotangent):
    slots, tile = tiles.shape[2], tiles.shape[-1]
    rows_dev, width = features.shape
    inner = 2 if n_row % 2 == 0 else 1
    near = 2 if n_col % 2 == 0 else 1
    outer = n_row // inner
    g_rows = width // n_col
    pieces = min(n_row, g_rows // 16)
    g_piece = g_rows // pieces
    src, dst = n_col * rows_dev, n_row * rows_dev
    dma = pltpu.SemaphoreType.DMA
    vmem = pl.BlockSpec(memory_space=pltpu.VMEM)
    smem = pl.BlockSpec(memory_space=pltpu.SMEM)
    buffers = [
        ((n_col, rows_dev, width), BF16),
        ((width, src), BF16),
        ((width, dst), BF16),
        ((n_row, rows_dev, width), BF16),
        ((slots + 1, tile, tile), BF16),
        ((slots + 1, tile, tile), BF16),
        ((dst, src), BF16),
        ((src, dst), BF16),
        ((width, width), BF16),
        ((width, width), BF16),
        ((src, width), BF16),
        ((outer, inner, rows_dev, width), F32),
        ((outer, inner, rows_dev, width), BF16),
        ((outer, inner, rows_dev, width), BF16),
        ((outer, rows_dev, width), BF16),
        ((src, width), F32),
        ((n_col, rows_dev, width), BF16),
        ((n_col, rows_dev, width), BF16),
        ((width, width), F32),
        ((n_col, g_rows, width), BF16),
        ((n_col, g_rows, width), BF16),
        ((pieces, g_piece, width), BF16),
        ((n_row, g_piece, width), BF16),
        ((n_col, pieces, g_piece, width), BF16),
    ]
    limit = sum(math.prod(shape) * jnp.dtype(kind).itemsize for shape, kind in buffers) + 12 * 2**20
    sems = [
        (n_col,), (n_col,), (outer,), (outer,), (outer + 1, inner), (n_row,), (outer, inner), (outer, inner),
        (outer,), (outer,), (n_col,), (n_col,), (n_col,), (n_col,), (n_row,), (n_row,),
        (n_row,), (n_row,), (n_col, pieces), (n_col, pieces), (n_col, pieces, near),
    ]
    aggregated, grad_x, grad_w = pl.pallas_call(
        functools.partial(layer_kernel, n_col, n_row, inner, near, pieces),
        out_shape=(
            jax.ShapeDtypeStruct((rows_dev, width), BF16),
            jax.ShapeDtypeStruct((rows_dev, width), F32),
            jax.ShapeDtypeStruct((width, width), BF16),
        ),
        in_specs=[smem] * 3 + [vmem] * 4,
        out_specs=(vmem, vmem, vmem),
        scratch_shapes=[pltpu.VMEM(shape, kind) for shape, kind in buffers] + [dma(s) for s in sems],
        compiler_params=pltpu.CompilerParams(
            collective_id=0, has_side_effects=True, vmem_limit_bytes=limit
        ),
        name="layer",
    )(
        tile_rows.reshape(slots), tile_cols.reshape(slots), tile_count.reshape(1),
        features, weight, tiles[0, 0], cotangent,
    )
    return pl.pallas_call(
        write_kernel,
        out_shape=(
            jax.ShapeDtypeStruct((rows_dev, width), BF16),
            jax.ShapeDtypeStruct((rows_dev, width), F32),
            jax.ShapeDtypeStruct((width, width), F32),
        ),
        in_specs=[vmem] * 3,
        out_specs=(vmem,) * 3,
        name="write",
    )(aggregated, grad_x, grad_w)


def solution(mesh):
    placed = (
        P(("row", "col"), None),
        P(),
        P("col", "row", None, None, None),
        P("col", "row", None),
        P("col", "row", None),
        P("col", "row"),
        P(("col", "row"), None),
    )
    return jax.shard_map(
        functools.partial(shards, mesh.shape["col"], mesh.shape["row"]),
        mesh=mesh,
        in_specs=placed,
        out_specs=(P(("col", "row"), None), P(("row", "col"), None), P()),
        check_vma=False,
    )
```

```python
import functools
import math

import jax
import jax.numpy as jnp
from jax import lax
from jax.experimental import pallas as pl
from jax.experimental.pallas import tpu as pltpu
from jax.sharding import PartitionSpec as P

BF16 = jnp.bfloat16
F32 = jnp.float32
MESH = pl.DeviceIdType.MESH


def each(count, body):
    if count <= 8:
        for step in range(count):
            body(step)
    else:
        lax.fori_loop(0, count, lambda step, _: (body(step), None)[1], None)


def matmul(a, b, contract=((1,), (0,))):
    return lax.dot_general(a, b, (contract, ((), ())), preferred_element_type=F32)


def layer_kernel(
    n_col, n_row, inner, near, pieces,
    rows_in, cols_in, count_in, feat_in, w_in, tiles_in, cot_ref,
    agg_ref, gx_ref, gw_ref,
    rows_ref, cols_ref, count_ref, feat_ref, w_ref, tiles_ref,
    feat_all, feat_t, ax_t, cot_all, pad, pad_t, a_ref, at_ref, w_hi, w_lo, proj, part, part_send, y_in, z_in,
    back, back_send, c_in, g_sum, g_part, g1_in, g1_sum, g2_in, gw_all,
    in_s, feat_s, feat_r, up_s, down_s, coty_s, cot_r, py_s, py_r, pz_s, pz_r, c_s, c_r,
    g1_s, g1_r, g2_s, g2_r, g3_s, g3_r, g4_s, g4_r, g5_s,
):
    outer = n_row // inner
    slots, tile = tiles_ref.shape[0], tiles_ref.shape[1]
    rows_dev, width = cot_ref.shape
    per_dev = rows_dev // tile
    dst_tiles, src_tiles = n_row * per_dev, n_col * per_dev
    col, row = lax.axis_index("col"), lax.axis_index("row")
    out_id, in_id = row // inner, row % inner
    g_rows = width // n_col
    g_piece = g_rows // pieces

    def send(src, dst, s_sem, r_sem, target):
        copy = pltpu.make_async_remote_copy(
            src_ref=src, dst_ref=dst, send_sem=s_sem, recv_sem=r_sem,
            device_id=target, device_id_type=MESH,
        )
        copy.start()

    def sent(ref, s_sem):
        pltpu.make_async_remote_copy(
            src_ref=ref, dst_ref=ref, send_sem=s_sem, recv_sem=s_sem,
            device_id={"col": col}, device_id_type=MESH,
        ).wait_send()

    def landed(ref, r_sem):
        pltpu.make_async_remote_copy(
            src_ref=ref, dst_ref=ref, send_sem=r_sem, recv_sem=r_sem,
            device_id={"col": col}, device_id_type=MESH,
        ).wait_recv()

    def col_at(d):
        return lax.rem(col + d, n_col)

    def row_at(d):
        return lax.rem(row + d, n_row)

    def out_at(d):
        return lax.rem(out_id + d, outer)

    def in_at(d):
        return lax.rem(in_id + d, inner)

    def reducer(r, body):
        if pieces == n_row:
            body()
        else:
            pl.when(r < pieces)(body)

    barrier = pltpu.get_barrier_semaphore()
    each(n_col - 1, lambda d: pl.semaphore_signal(
        barrier, inc=1, device_id={"col": col_at(d + 1)}, device_id_type=MESH))
    each(n_row - 1, lambda d: pl.semaphore_signal(
        barrier, inc=1, device_id={"row": row_at(d + 1)}, device_id_type=MESH))
    fetches = [
        pltpu.make_async_copy(source, target, in_s.at[k])
        for k, (source, target) in enumerate((
            (cot_ref, cot_all.at[row]), (feat_in, feat_ref), (tiles_in, tiles_ref),
            (rows_in, rows_ref), (cols_in, cols_ref), (count_in, count_ref), (w_in, w_ref),
        ))
    ]
    for fetch in fetches:
        fetch.start()
    fetches[1].wait()
    feat_all[col] = feat_ref[...].astype(BF16)
    fetches[0].wait()
    pl.semaphore_wait(barrier, n_col + n_row - 2)

    def chain(o, step, sems, d):
        slot = o * inner + in_id
        to = out_id + step
        send(cot_all.at[slot], cot_all.at[slot], sems.at[d], cot_r.at[slot], {"row": to * inner + in_id})

    def cot_forward(o, d_out):
        def one(d):
            slot = o * inner + in_id
            send(cot_all.at[slot], cot_all.at[slot], coty_s.at[d_out, d], cot_r.at[slot],
                 {"row": out_id * inner + in_at(d + 1)})
        each(inner - 1, one)

    if outer > 1:
        pl.when(out_id < outer - 1)(lambda: chain(out_id, 1, up_s, 0))
        pl.when(out_id > 0)(lambda: chain(out_id, -1, down_s, 0))
    cot_forward(out_id, 0)

    def feat_out(d):
        send(feat_all.at[col], feat_all.at[col], feat_s.at[d], feat_r.at[col], {"col": col_at(d + 1)})

    each(n_col - 1, feat_out)

    def pad_one(t):
        one = tiles_ref[t]
        pad[t] = one
        pad_t[t] = one.T

    for fetch in fetches[2:]:
        fetch.wait()
    each(slots, pad_one)
    pad[slots] = jnp.zeros((tile, tile), BF16)
    pad_t[slots] = jnp.zeros((tile, tile), BF16)
    live = count_ref[0, 0]
    places = [
        jnp.where(t < live, rows_ref[0, 0, t] * src_tiles + cols_ref[0, 0, t], -1) for t in range(slots)
    ]

    def lay(i):
        for k in range(src_tiles):
            index = jnp.int32(slots)
            for t in range(slots):
                index = jnp.where(places[t] == i * src_tiles + k, t, index)
            at = i * tile if isinstance(i, int) else pl.multiple_of(i * tile, tile)
            a_ref[pl.ds(at, tile), k * tile:(k + 1) * tile] = pad[index]
            at_ref[k * tile:(k + 1) * tile, pl.ds(at, tile)] = pad_t[index]

    each(dst_tiles, lay)
    weight = w_ref[...]
    w_hi[...] = weight.astype(BF16)
    w_lo[...] = (weight - w_hi[...].astype(F32)).astype(BF16)

    def project(d):
        c = col_at(d)
        if not (isinstance(d, int) and d == 0):
            landed(feat_all.at[c], feat_r.at[c])
        block = feat_all[c]
        at = pl.multiple_of(c * rows_dev, rows_dev)
        proj[pl.ds(at, rows_dev), :] = (
            matmul(block, w_hi[...]) + matmul(block, w_lo[...])
        ).astype(BF16)
        feat_t[:, pl.ds(at, rows_dev)] = block.T

    project(0)

    def pass_on(d):
        def from_below():
            o = out_id - d
            landed(cot_all.at[o * inner + in_id], cot_r.at[o * inner + in_id])
            pl.when(out_id < outer - 1)(lambda: chain(o, 1, up_s, d))
            cot_forward(o, o + 1)

        def from_above():
            o = out_id + d
            landed(cot_all.at[o * inner + in_id], cot_r.at[o * inner + in_id])
            pl.when(out_id > 0)(lambda: chain(o, -1, down_s, d))
            cot_forward(o, o + 1)

        pl.when(out_id - d >= 0)(from_below)
        pl.when(out_id + d < outer)(from_above)

    span = inner * rows_dev

    def forward(o):
        at = o * span if isinstance(o, int) else pl.multiple_of(o * span, span)
        result = matmul(a_ref[pl.ds(at, span), :], proj[...]).reshape(inner, rows_dev, width)
        part[o] = result
        part_send[o] = result.astype(BF16)

    def weight_term(d):
        def add(o):
            def one(e):
                slot = o * inner + in_at(e + 1)
                landed(cot_all.at[slot], cot_r.at[slot])
            each(inner - 1, one)
            block = ax_t[:, pl.ds(pl.multiple_of(o * span, span), span)]
            g_sum[...] += matmul(block, cot_all[pl.ds(o * inner, inner)].reshape(span, width))

        if isinstance(d, int) and d == 0:
            add(out_id)
        else:
            pl.when(out_id - d >= 0)(lambda: add(out_id - d))
            pl.when(out_id + d < outer)(lambda: add(out_id + d))

    def inner_out(d):
        o = out_at(d + 1)

        def one(e):
            target = in_at(e + 1)
            send(part_send.at[o, target], y_in.at[o, in_id], py_s.at[o, e], py_r.at[o, in_id],
                 {"row": out_id * inner + target})
        each(inner - 1, one)

    if outer > 1:
        pass_on(1)
    each(n_col - 1, lambda d: project(d + 1))
    each(min(outer - 2, 1), lambda d: pass_on(2))
    each(outer, forward)
    each(outer - 3, lambda d: pass_on(d + 3))
    first = outer // 2
    each(first, inner_out)
    ax_t[...] = matmul(feat_t[...], at_ref[...]).astype(BF16)
    g_sum[...] = jnp.zeros_like(g_sum)
    weight_term(0)
    each(outer - 1, lambda d: weight_term(d + 1))
    g_part[...] = g_sum[...].astype(BF16).reshape(n_col, g_rows, width)

    def g1_out(d):
        c = col_at(d + 1)
        send(g_part.at[c], g1_in.at[col], g1_s.at[d], g1_r.at[col], {"col": c})

    each(n_col - 1, g1_out)
    each(outer - first, lambda d: inner_out(d + first))

    back[...] = matmul(at_ref[...], cot_all[...].reshape(n_row * rows_dev, width))
    back_send[...] = back[...].astype(BF16).reshape(n_col, rows_dev, width)

    def c_out(d):
        c = col_at(d + 1)
        send(back_send.at[c], c_in.at[col], c_s.at[d], c_r.at[col], {"col": c})

    def inner_sum(o):
        def one(e):
            source = in_at(e + 1)
            landed(y_in.at[o, source], py_r.at[o, source])
            part[o, in_id] += y_in[o, source].astype(F32)
        each(inner - 1, one)

    def outer_out(d):
        o = out_at(d + 1)
        inner_sum(o)
        part_send[o, in_id] = part[o, in_id].astype(BF16)
        send(part_send.at[o, in_id], z_in.at[out_id], pz_s.at[d], pz_r.at[out_id], {"row": o * inner + in_id})

    each(outer - 1, outer_out)

    gw_part = g_part[col].astype(F32)
    def g1_add(d, total):
        c = col_at(d + 1)
        landed(g1_in.at[c], g1_r.at[c])
        return total + g1_in[c].astype(F32)
    for d in range(n_col - 1):
        gw_part = g1_add(d, gw_part)
    g1_sum[...] = gw_part.astype(BF16).reshape(pieces, g_piece, width)

    def g2_out(d):
        r = row_at(d + 1)
        reducer(r, lambda: send(g1_sum.at[r], g2_in.at[row], g2_s.at[d], g2_r.at[row], {"row": r}))

    each(n_row - 1, g2_out)
    each(n_col - 1, c_out)

    inner_sum(out_id)

    def g2_sum():
        def g2_wait(d):
            r = row_at(d + 1)
            landed(g2_in.at[r], g2_r.at[r])
        each(n_row - 1, g2_wait)
        g2_in[row] = g1_sum[row]
        total = g2_in[0].astype(F32)
        for r in range(1, n_row):
            total = total + g2_in[r].astype(F32)
        gw_all[col, row] = total.astype(BF16)

        def g3_out(d):
            send(gw_all.at[col, row], gw_all.at[col, row], g3_s.at[d], g3_r.at[row], {"row": row_at(d + 1)})
        each(n_row - 1, g3_out)

    reducer(row, g2_sum)

    def z_wait(d):
        o = out_at(d + 1)
        landed(z_in.at[o], pz_r.at[o])
        part[out_id, in_id] += z_in[o].astype(F32)

    each(outer - 1, z_wait)
    agg_ref[...] = part[out_id, in_id].astype(BF16)

    def outer_col(d):
        return lax.rem(col // near + d, n_col // near) * near + col % near

    def near_col(d):
        return col // near * near + lax.rem(col % near + d, near)

    def to_near(c, r, d):
        def one(e):
            send(gw_all.at[c, r], gw_all.at[c, r], g5_s.at[d, r, e], g4_r.at[c, r], {"col": near_col(e + 1)})
        each(near - 1, one)

    def piece_out(r):
        def one(d):
            send(gw_all.at[col, r], gw_all.at[col, r], g4_s.at[d, r], g4_r.at[col, r], {"col": outer_col(d + 1)})
        each(n_col // near - 1, one)
        to_near(col, r, 0)

    def g3_wait(d):
        r = row_at(d + 1)

        def piece():
            landed(gw_all.at[col, r], g3_r.at[r])
            piece_out(r)
        reducer(r, piece)

    reducer(row, lambda: piece_out(row))
    each(n_row - 1, g3_wait)

    def c_add(d):
        c = col_at(d + 1)
        landed(c_in.at[c], c_r.at[c])
    each(n_col - 1, c_add)
    grad_y = back[pl.ds(pl.multiple_of(col * rows_dev, rows_dev), rows_dev), :]
    for d in range(n_col - 1):
        grad_y = grad_y + c_in[col_at(d + 1)].astype(F32)
    grad_y = grad_y.astype(BF16)
    gx_ref[...] = matmul(grad_y, w_hi[...], ((1,), (1,))) + matmul(grad_y, w_lo[...], ((1,), (1,)))

    def pass_piece(d):
        c = outer_col(d + 1)

        def one(e):
            r = row_at(e)

            def piece():
                landed(gw_all.at[c, r], g4_r.at[c, r])
                to_near(c, r, d + 1)
            reducer(r, piece)
        each(n_row, one)

    each(n_col // near - 1, pass_piece)

    def last_wait(d):
        def one(e):
            c = near_col(e + 1)
            c = lax.rem(c // near + d, n_col // near) * near + c % near
            each(pieces, lambda r: landed(gw_all.at[c, r], g4_r.at[c, r]))
        each(near - 1, one)

    each(n_col // near, last_wait)
    gw_ref[...] = gw_all[...].reshape(width, width)

    each(n_col - 1, lambda d: sent(feat_all.at[0], feat_s.at[d]))
    def chain_sent(d):
        def up():
            sent(cot_ref, up_s.at[d])

        def down():
            sent(cot_ref, down_s.at[d])
        pl.when((out_id - d >= 0) & (out_id < outer - 1))(up)
        pl.when((out_id + d < outer) & (out_id > 0))(down)

    if outer > 1:
        each(outer, chain_sent)
    each(outer, lambda o: each(inner - 1, lambda e: sent(
        cot_ref, coty_s.at[jnp.where(out_id == o, 0, o + 1), e])))
    each(outer, lambda d: each(inner - 1, lambda e: sent(y_in.at[0, 0], py_s.at[d, e])))
    each(outer - 1, lambda d: sent(z_in.at[0], pz_s.at[d]))
    each(n_col - 1, lambda d: sent(c_in.at[0], c_s.at[d]))
    each(n_col - 1, lambda d: sent(g1_in.at[0], g1_s.at[d]))
    each(n_row - 1, lambda d: reducer(row_at(d + 1), lambda: sent(g2_in.at[0], g2_s.at[d])))
    reducer(row, lambda: each(n_row - 1, lambda d: sent(g2_in.at[0], g3_s.at[d])))
    each(pieces, lambda r: each(n_col // near - 1, lambda d: sent(g2_in.at[0], g4_s.at[d, r])))
    each(pieces, lambda r: each(n_col // near, lambda d: each(
        near - 1, lambda e: sent(g2_in.at[0], g5_s.at[d, r, e]))))


def write_kernel(agg_ref, gx_ref, gw_ref, agg_out, gx_out, gw_out, narrow, wide, sems):
    copies = [
        pltpu.make_async_copy(agg_ref, agg_out, sems.at[0]),
        pltpu.make_async_copy(gx_ref, gx_out, sems.at[1]),
    ]
    load = pltpu.make_async_copy(gw_ref, narrow, sems.at[2])
    load.start()
    for copy in copies:
        copy.start()
    load.wait()
    wide[...] = narrow[...].astype(F32)
    store = pltpu.make_async_copy(wide, gw_out, sems.at[3])
    store.start()
    for copy in copies + [store]:
        copy.wait()


def shards(n_col, n_row, features, weight, tiles, tile_rows, tile_cols, tile_count, cotangent):
    slots, tile = tiles.shape[2], tiles.shape[-1]
    rows_dev, width = features.shape
    inner = 2 if n_row % 2 == 0 else 1
    near = 2 if n_col % 2 == 0 else 1
    outer = n_row // inner
    g_rows = width // n_col
    pieces = min(n_row, g_rows // 16)
    g_piece = g_rows // pieces
    src, dst = n_col * rows_dev, n_row * rows_dev
    dma = pltpu.SemaphoreType.DMA
    vmem = pl.BlockSpec(memory_space=pltpu.VMEM)
    hbm = pl.BlockSpec(memory_space=pltpu.HBM)
    anywhere = pl.BlockSpec(memory_space=pl.ANY)
    buffers = [
        (features.shape, F32),
        (weight.shape, F32),
        (tiles.shape[2:], BF16),
        ((n_col, rows_dev, width), BF16),
        ((width, src), BF16),
        ((width, dst), BF16),
        ((n_row, rows_dev, width), BF16),
        ((slots + 1, tile, tile), BF16),
        ((slots + 1, tile, tile), BF16),
        ((dst, src), BF16),
        ((src, dst), BF16),
        ((width, width), BF16),
        ((width, width), BF16),
        ((src, width), BF16),
        ((outer, inner, rows_dev, width), F32),
        ((outer, inner, rows_dev, width), BF16),
        ((outer, inner, rows_dev, width), BF16),
        ((outer, rows_dev, width), BF16),
        ((src, width), F32),
        ((n_col, rows_dev, width), BF16),
        ((n_col, rows_dev, width), BF16),
        ((width, width), F32),
        ((n_col, g_rows, width), BF16),
        ((n_col, g_rows, width), BF16),
        ((pieces, g_piece, width), BF16),
        ((n_row, g_piece, width), BF16),
        ((n_col, pieces, g_piece, width), BF16),
    ]
    held = sum(math.prod(shape) * jnp.dtype(kind).itemsize for shape, kind in buffers)
    limit = max(56 * 2**20, min(held + 12 * 2**20, 63 * 2**20))
    sems = [
        (7,), (n_col,), (n_col,), (outer,), (outer,), (outer + 1, inner), (n_row,), (outer, inner), (outer, inner),
        (outer,), (outer,), (n_col,), (n_col,), (n_col,), (n_col,), (n_row,), (n_row,),
        (n_row,), (n_row,), (n_col, pieces), (n_col, pieces), (n_col, pieces, near),
    ]
    aggregated, grad_x, grad_w = pl.pallas_call(
        functools.partial(layer_kernel, n_col, n_row, inner, near, pieces),
        out_shape=(
            jax.ShapeDtypeStruct((rows_dev, width), BF16),
            jax.ShapeDtypeStruct((rows_dev, width), F32),
            jax.ShapeDtypeStruct((width, width), BF16),
        ),
        in_specs=[hbm] * 7,
        out_specs=(vmem, vmem, vmem),
        scratch_shapes=[pltpu.SMEM(one.shape, jnp.int32) for one in (tile_rows, tile_cols, tile_count)]
        + [pltpu.VMEM(shape, kind) for shape, kind in buffers] + [dma(s) for s in sems],
        compiler_params=pltpu.CompilerParams(
            collective_id=0, has_side_effects=True, vmem_limit_bytes=limit
        ),
        name="layer",
    )(
        tile_rows, tile_cols, tile_count,
        features, weight, tiles[0, 0], cotangent,
    )
    return pl.pallas_call(
        write_kernel,
        out_shape=(
            jax.ShapeDtypeStruct((rows_dev, width), BF16),
            jax.ShapeDtypeStruct((rows_dev, width), F32),
            jax.ShapeDtypeStruct((width, width), F32),
        ),
        in_specs=[anywhere] * 3,
        out_specs=(hbm,) * 3,
        scratch_shapes=[
            pltpu.VMEM((width, width), BF16), pltpu.VMEM((width, width), F32), dma((4,)),
        ],
        compiler_params=pltpu.CompilerParams(vmem_limit_bytes=limit),
        name="write",
    )(aggregated, grad_x, grad_w)


def solution(mesh):
    placed = (
        P(("row", "col"), None),
        P(),
        P("col", "row", None, None, None),
        P("col", "row", None),
        P("col", "row", None),
        P("col", "row"),
        P(("col", "row"), None),
    )
    return jax.shard_map(
        functools.partial(shards, mesh.shape["col"], mesh.shape["row"]),
        mesh=mesh,
        in_specs=placed,
        out_specs=(P(("col", "row"), None), P(("row", "col"), None), P()),
        check_vma=False,
    )
```

```python
import functools
import math

import jax
import jax.numpy as jnp
from jax import lax
from jax.experimental import pallas as pl
from jax.experimental.pallas import tpu as pltpu
from jax.sharding import PartitionSpec as P

BF16 = jnp.bfloat16
F32 = jnp.float32
MESH = pl.DeviceIdType.MESH


def each(count, body):
    if count <= 8:
        for step in range(count):
            body(step)
    else:
        lax.fori_loop(0, count, lambda step, _: (body(step), None)[1], None)


def matmul(a, b, contract=((1,), (0,))):
    return lax.dot_general(a, b, (contract, ((), ())), preferred_element_type=F32)


def layer_kernel(
    n_col, n_row, inner, near, pieces,
    rows_in, cols_in, count_in, feat_in, w_in, tiles_in, cot_ref,
    agg_ref, gx_ref, gw_ref,
    rows_ref, cols_ref, count_ref, feat_ref, w_ref, tiles_ref,
    feat_all, feat_t, ax_t, cot_all, pad, pad_t, a_ref, at_ref, w_hi, w_lo, proj, part, part_send, y_in, z_in,
    back, back_send, c_in, g_sum, g_part, g1_in, g1_sum, g2_in, gw_all,
    in_s, feat_s, feat_r, up_s, down_s, coty_s, cot_r, py_s, py_r, pz_s, pz_r, c_s, c_r,
    g1_s, g1_r, g2_s, g2_r, g3_s, g3_r, g4_s, g4_r, g5_s,
):
    outer = n_row // inner
    slots, tile = tiles_ref.shape[0], tiles_ref.shape[1]
    rows_dev, width = cot_ref.shape
    per_dev = rows_dev // tile
    dst_tiles, src_tiles = n_row * per_dev, n_col * per_dev
    col, row = lax.axis_index("col"), lax.axis_index("row")
    out_id, in_id = row // inner, row % inner
    g_rows = width // n_col
    g_piece = g_rows // pieces

    def send(src, dst, s_sem, r_sem, target):
        copy = pltpu.make_async_remote_copy(
            src_ref=src, dst_ref=dst, send_sem=s_sem, recv_sem=r_sem,
            device_id=target, device_id_type=MESH,
        )
        copy.start()

    def sent(ref, s_sem):
        pltpu.make_async_remote_copy(
            src_ref=ref, dst_ref=ref, send_sem=s_sem, recv_sem=s_sem,
            device_id={"col": col}, device_id_type=MESH,
        ).wait_send()

    def landed(ref, r_sem):
        pltpu.make_async_remote_copy(
            src_ref=ref, dst_ref=ref, send_sem=r_sem, recv_sem=r_sem,
            device_id={"col": col}, device_id_type=MESH,
        ).wait_recv()

    def col_at(d):
        return lax.rem(col + d, n_col)

    def row_at(d):
        return lax.rem(row + d, n_row)

    def out_at(d):
        return lax.rem(out_id + d, outer)

    def in_at(d):
        return lax.rem(in_id + d, inner)

    def reducer(r, body):
        if pieces == n_row:
            body()
        else:
            pl.when(r < pieces)(body)

    barrier = pltpu.get_barrier_semaphore()
    each(n_col - 1, lambda d: pl.semaphore_signal(
        barrier, inc=1, device_id={"col": col_at(d + 1)}, device_id_type=MESH))
    each(n_row - 1, lambda d: pl.semaphore_signal(
        barrier, inc=1, device_id={"row": row_at(d + 1)}, device_id_type=MESH))
    fetches = [
        pltpu.make_async_copy(source, target, in_s.at[k])
        for k, (source, target) in enumerate((
            (cot_ref, cot_all.at[row]), (feat_in, feat_ref), (tiles_in, tiles_ref),
            (rows_in, rows_ref), (cols_in, cols_ref), (count_in, count_ref), (w_in, w_ref),
        ))
    ]
    for fetch in fetches:
        fetch.start()
    fetches[1].wait()
    feat_all[col] = feat_ref[...].astype(BF16)
    fetches[0].wait()
    pl.semaphore_wait(barrier, n_col + n_row - 2)

    def chain(o, step, sems, d):
        slot = o * inner + in_id
        to = out_id + step
        send(cot_all.at[slot], cot_all.at[slot], sems.at[d], cot_r.at[slot], {"row": to * inner + in_id})

    def cot_forward(o, d_out):
        def one(d):
            slot = o * inner + in_id
            send(cot_all.at[slot], cot_all.at[slot], coty_s.at[d_out, d], cot_r.at[slot],
                 {"row": out_id * inner + in_at(d + 1)})
        each(inner - 1, one)

    if outer > 1:
        pl.when(out_id < outer - 1)(lambda: chain(out_id, 1, up_s, 0))
        pl.when(out_id > 0)(lambda: chain(out_id, -1, down_s, 0))
    cot_forward(out_id, 0)

    def feat_out(d):
        send(feat_all.at[col], feat_all.at[col], feat_s.at[d], feat_r.at[col], {"col": col_at(d + 1)})

    each(n_col - 1, feat_out)

    def pad_one(t):
        one = tiles_ref[t]
        pad[t] = one
        pad_t[t] = one.T

    for fetch in fetches[2:]:
        fetch.wait()
    each(slots, pad_one)
    pad[slots] = jnp.zeros((tile, tile), BF16)
    pad_t[slots] = jnp.zeros((tile, tile), BF16)
    live = count_ref[0, 0]
    places = [
        jnp.where(t < live, rows_ref[0, 0, t] * src_tiles + cols_ref[0, 0, t], -1) for t in range(slots)
    ]

    def lay(i):
        for k in range(src_tiles):
            index = jnp.int32(slots)
            for t in range(slots):
                index = jnp.where(places[t] == i * src_tiles + k, t, index)
            at = i * tile if isinstance(i, int) else pl.multiple_of(i * tile, tile)
            a_ref[pl.ds(at, tile), k * tile:(k + 1) * tile] = pad[index]
            at_ref[k * tile:(k + 1) * tile, pl.ds(at, tile)] = pad_t[index]

    each(dst_tiles, lay)
    weight = w_ref[...]
    w_hi[...] = weight.astype(BF16)
    w_lo[...] = (weight - w_hi[...].astype(F32)).astype(BF16)

    def project(d):
        c = col_at(d)
        if not (isinstance(d, int) and d == 0):
            landed(feat_all.at[c], feat_r.at[c])
        block = feat_all[c]
        at = pl.multiple_of(c * rows_dev, rows_dev)
        proj[pl.ds(at, rows_dev), :] = (
            matmul(block, w_hi[...]) + matmul(block, w_lo[...])
        ).astype(BF16)
        feat_t[:, pl.ds(at, rows_dev)] = block.T

    project(0)

    def pass_on(d):
        def from_below():
            o = out_id - d
            landed(cot_all.at[o * inner + in_id], cot_r.at[o * inner + in_id])
            pl.when(out_id < outer - 1)(lambda: chain(o, 1, up_s, d))
            cot_forward(o, o + 1)

        def from_above():
            o = out_id + d
            landed(cot_all.at[o * inner + in_id], cot_r.at[o * inner + in_id])
            pl.when(out_id > 0)(lambda: chain(o, -1, down_s, d))
            cot_forward(o, o + 1)

        pl.when(out_id - d >= 0)(from_below)
        pl.when(out_id + d < outer)(from_above)

    span = inner * rows_dev

    def forward(o):
        at = o * span if isinstance(o, int) else pl.multiple_of(o * span, span)
        result = matmul(a_ref[pl.ds(at, span), :], proj[...]).reshape(inner, rows_dev, width)
        part[o] = result
        part_send[o] = result.astype(BF16)

    def weight_term(k, _):
        o = out_id + jnp.where(k % 2 == 1, -((k + 1) // 2), k // 2)

        def add():
            def one(e):
                slot = o * inner + in_at(e + 1)
                landed(cot_all.at[slot], cot_r.at[slot])
            each(inner - 1, one)
            block = ax_t[:, pl.ds(pl.multiple_of(o * span, span), span)]
            g_sum[...] += matmul(block, cot_all[pl.ds(o * inner, inner)].reshape(span, width))

        pl.when((o >= 0) & (o < outer))(add)

    def inner_out(d):
        o = out_at(d + 1)

        def one(e):
            target = in_at(e + 1)
            send(part_send.at[o, target], y_in.at[o, in_id], py_s.at[o, e], py_r.at[o, in_id],
                 {"row": out_id * inner + target})
        each(inner - 1, one)

    if outer > 1:
        pass_on(1)
    each(n_col - 1, lambda d: project(d + 1))
    each(min(outer - 2, 1), lambda d: pass_on(2))
    lax.fori_loop(0, outer, lambda o, _: forward(o), None)
    each(outer - 3, lambda d: pass_on(d + 3))
    first = outer // 2
    each(first, inner_out)
    ax_t[...] = matmul(feat_t[...], at_ref[...]).astype(BF16)
    g_sum[...] = jnp.zeros_like(g_sum)
    lax.fori_loop(0, 2 * outer - 1, weight_term, None)
    g_part[...] = g_sum[...].astype(BF16).reshape(n_col, g_rows, width)

    def g1_out(d):
        c = col_at(d + 1)
        send(g_part.at[c], g1_in.at[col], g1_s.at[d], g1_r.at[col], {"col": c})

    each(n_col - 1, g1_out)
    each(outer - first, lambda d: inner_out(d + first))

    back[...] = matmul(at_ref[...], cot_all[...].reshape(n_row * rows_dev, width))
    back_send[...] = back[...].astype(BF16).reshape(n_col, rows_dev, width)

    def c_out(d):
        c = col_at(d + 1)
        send(back_send.at[c], c_in.at[col], c_s.at[d], c_r.at[col], {"col": c})

    def inner_sum(o):
        def one(e):
            source = in_at(e + 1)
            landed(y_in.at[o, source], py_r.at[o, source])
            part[o, in_id] += y_in[o, source].astype(F32)
        each(inner - 1, one)

    def outer_out(d):
        o = out_at(d + 1)
        inner_sum(o)
        part_send[o, in_id] = part[o, in_id].astype(BF16)
        send(part_send.at[o, in_id], z_in.at[out_id], pz_s.at[d], pz_r.at[out_id], {"row": o * inner + in_id})

    each(outer - 1, outer_out)

    gw_part = g_part[col].astype(F32)
    def g1_add(d, total):
        c = col_at(d + 1)
        landed(g1_in.at[c], g1_r.at[c])
        return total + g1_in[c].astype(F32)
    for d in range(n_col - 1):
        gw_part = g1_add(d, gw_part)
    g1_sum[...] = gw_part.astype(BF16).reshape(pieces, g_piece, width)

    def g2_out(d):
        r = row_at(d + 1)
        reducer(r, lambda: send(g1_sum.at[r], g2_in.at[row], g2_s.at[d], g2_r.at[row], {"row": r}))

    each(n_row - 1, g2_out)
    each(n_col - 1, c_out)

    inner_sum(out_id)

    def g2_sum():
        def g2_wait(d):
            r = row_at(d + 1)
            landed(g2_in.at[r], g2_r.at[r])
        each(n_row - 1, g2_wait)
        g2_in[row] = g1_sum[row]
        total = g2_in[0].astype(F32)
        for r in range(1, n_row):
            total = total + g2_in[r].astype(F32)
        gw_all[col, row] = total.astype(BF16)

        def g3_out(d):
            send(gw_all.at[col, row], gw_all.at[col, row], g3_s.at[d], g3_r.at[row], {"row": row_at(d + 1)})
        each(n_row - 1, g3_out)

    reducer(row, g2_sum)

    def z_wait(d):
        o = out_at(d + 1)
        landed(z_in.at[o], pz_r.at[o])
        part[out_id, in_id] += z_in[o].astype(F32)

    each(outer - 1, z_wait)
    agg_ref[...] = part[out_id, in_id].astype(BF16)

    def outer_col(d):
        return lax.rem(col // near + d, n_col // near) * near + col % near

    def near_col(d):
        return col // near * near + lax.rem(col % near + d, near)

    def to_near(c, r, d):
        def one(e):
            send(gw_all.at[c, r], gw_all.at[c, r], g5_s.at[d, r, e], g4_r.at[c, r], {"col": near_col(e + 1)})
        each(near - 1, one)

    def piece_out(r):
        def one(d):
            send(gw_all.at[col, r], gw_all.at[col, r], g4_s.at[d, r], g4_r.at[col, r], {"col": outer_col(d + 1)})
        each(n_col // near - 1, one)
        to_near(col, r, 0)

    def g3_wait(d):
        r = row_at(d + 1)

        def piece():
            landed(gw_all.at[col, r], g3_r.at[r])
            piece_out(r)
        reducer(r, piece)

    reducer(row, lambda: piece_out(row))
    each(n_row - 1, g3_wait)

    def c_add(d):
        c = col_at(d + 1)
        landed(c_in.at[c], c_r.at[c])
    each(n_col - 1, c_add)
    grad_y = back[pl.ds(pl.multiple_of(col * rows_dev, rows_dev), rows_dev), :]
    for d in range(n_col - 1):
        grad_y = grad_y + c_in[col_at(d + 1)].astype(F32)
    grad_y = grad_y.astype(BF16)
    gx_ref[...] = matmul(grad_y, w_hi[...], ((1,), (1,))) + matmul(grad_y, w_lo[...], ((1,), (1,)))

    def pass_piece(d):
        c = outer_col(d + 1)

        def one(e):
            r = row_at(e)

            def piece():
                landed(gw_all.at[c, r], g4_r.at[c, r])
                to_near(c, r, d + 1)
            reducer(r, piece)
        each(n_row, one)

    each(n_col // near - 1, pass_piece)

    def last_wait(d):
        def one(e):
            c = near_col(e + 1)
            c = lax.rem(c // near + d, n_col // near) * near + c % near
            each(pieces, lambda r: landed(gw_all.at[c, r], g4_r.at[c, r]))
        each(near - 1, one)

    each(n_col // near, last_wait)
    gw_ref[...] = gw_all[...].reshape(width, width)

    each(n_col - 1, lambda d: sent(feat_all.at[0], feat_s.at[d]))
    def chain_sent(d):
        def up():
            sent(cot_ref, up_s.at[d])

        def down():
            sent(cot_ref, down_s.at[d])
        pl.when((out_id - d >= 0) & (out_id < outer - 1))(up)
        pl.when((out_id + d < outer) & (out_id > 0))(down)

    if outer > 1:
        each(outer, chain_sent)
    each(outer, lambda o: each(inner - 1, lambda e: sent(
        cot_ref, coty_s.at[jnp.where(out_id == o, 0, o + 1), e])))
    each(outer, lambda d: each(inner - 1, lambda e: sent(y_in.at[0, 0], py_s.at[d, e])))
    each(outer - 1, lambda d: sent(z_in.at[0], pz_s.at[d]))
    each(n_col - 1, lambda d: sent(c_in.at[0], c_s.at[d]))
    each(n_col - 1, lambda d: sent(g1_in.at[0], g1_s.at[d]))
    each(n_row - 1, lambda d: reducer(row_at(d + 1), lambda: sent(g2_in.at[0], g2_s.at[d])))
    reducer(row, lambda: each(n_row - 1, lambda d: sent(g2_in.at[0], g3_s.at[d])))
    each(pieces, lambda r: each(n_col // near - 1, lambda d: sent(g2_in.at[0], g4_s.at[d, r])))
    each(pieces, lambda r: each(n_col // near, lambda d: each(
        near - 1, lambda e: sent(g2_in.at[0], g5_s.at[d, r, e]))))


def write_kernel(agg_ref, gx_ref, gw_ref, agg_out, gx_out, gw_out, agg, gx, narrow, wide, sems):
    loads = [
        pltpu.make_async_copy(source, target, sems.at[k])
        for k, (source, target) in enumerate(((gw_ref, narrow), (agg_ref, agg), (gx_ref, gx)))
    ]
    stores = [
        pltpu.make_async_copy(source, target, sems.at[3 + k])
        for k, (source, target) in enumerate(((wide, gw_out), (agg, agg_out), (gx, gx_out)))
    ]
    for load in loads:
        load.start()
    for k in (1, 2):
        loads[k].wait()
        stores[k].start()
    loads[0].wait()
    wide[...] = narrow[...].astype(F32)
    for k in (0, 1, 2):
        if k == 0:
            stores[k].start()
        stores[k].wait()


def shards(n_col, n_row, features, weight, tiles, tile_rows, tile_cols, tile_count, cotangent):
    slots, tile = tiles.shape[2], tiles.shape[-1]
    rows_dev, width = features.shape
    inner = 2 if n_row % 2 == 0 else 1
    near = 2 if n_col % 2 == 0 else 1
    outer = n_row // inner
    g_rows = width // n_col
    pieces = min(n_row, g_rows // 16)
    g_piece = g_rows // pieces
    src, dst = n_col * rows_dev, n_row * rows_dev
    dma = pltpu.SemaphoreType.DMA
    vmem = pl.BlockSpec(memory_space=pltpu.VMEM)
    hbm = pl.BlockSpec(memory_space=pltpu.HBM)
    anywhere = pl.BlockSpec(memory_space=pl.ANY)
    buffers = [
        (features.shape, F32),
        (weight.shape, F32),
        (tiles.shape[2:], BF16),
        ((n_col, rows_dev, width), BF16),
        ((width, src), BF16),
        ((width, dst), BF16),
        ((n_row, rows_dev, width), BF16),
        ((slots + 1, tile, tile), BF16),
        ((slots + 1, tile, tile), BF16),
        ((dst, src), BF16),
        ((src, dst), BF16),
        ((width, width), BF16),
        ((width, width), BF16),
        ((src, width), BF16),
        ((outer, inner, rows_dev, width), F32),
        ((outer, inner, rows_dev, width), BF16),
        ((outer, inner, rows_dev, width), BF16),
        ((outer, rows_dev, width), BF16),
        ((src, width), F32),
        ((n_col, rows_dev, width), BF16),
        ((n_col, rows_dev, width), BF16),
        ((width, width), F32),
        ((n_col, g_rows, width), BF16),
        ((n_col, g_rows, width), BF16),
        ((pieces, g_piece, width), BF16),
        ((n_row, g_piece, width), BF16),
        ((n_col, pieces, g_piece, width), BF16),
    ]
    held = sum(math.prod(shape) * jnp.dtype(kind).itemsize for shape, kind in buffers)
    limit = max(56 * 2**20, min(held + 12 * 2**20, 63 * 2**20))
    sems = [
        (7,), (n_col,), (n_col,), (outer,), (outer,), (outer + 1, inner), (n_row,), (outer, inner), (outer, inner),
        (outer,), (outer,), (n_col,), (n_col,), (n_col,), (n_col,), (n_row,), (n_row,),
        (n_row,), (n_row,), (n_col, pieces), (n_col, pieces), (n_col, pieces, near),
    ]
    aggregated, grad_x, grad_w = pl.pallas_call(
        functools.partial(layer_kernel, n_col, n_row, inner, near, pieces),
        out_shape=(
            jax.ShapeDtypeStruct((rows_dev, width), BF16),
            jax.ShapeDtypeStruct((rows_dev, width), F32),
            jax.ShapeDtypeStruct((width, width), BF16),
        ),
        in_specs=[hbm] * 7,
        out_specs=(vmem, vmem, vmem),
        scratch_shapes=[pltpu.SMEM(one.shape, jnp.int32) for one in (tile_rows, tile_cols, tile_count)]
        + [pltpu.VMEM(shape, kind) for shape, kind in buffers] + [dma(s) for s in sems],
        compiler_params=pltpu.CompilerParams(
            collective_id=0, has_side_effects=True, vmem_limit_bytes=limit
        ),
        name="layer",
    )(
        tile_rows, tile_cols, tile_count,
        features, weight, tiles[0, 0], cotangent,
    )
    return pl.pallas_call(
        write_kernel,
        out_shape=(
            jax.ShapeDtypeStruct((rows_dev, width), BF16),
            jax.ShapeDtypeStruct((rows_dev, width), F32),
            jax.ShapeDtypeStruct((width, width), F32),
        ),
        in_specs=[anywhere] * 3,
        out_specs=(hbm,) * 3,
        scratch_shapes=[
            pltpu.VMEM((rows_dev, width), BF16), pltpu.VMEM((rows_dev, width), F32),
            pltpu.VMEM((width, width), BF16), pltpu.VMEM((width, width), F32), dma((6,)),
        ],
        compiler_params=pltpu.CompilerParams(vmem_limit_bytes=limit),
        name="write",
    )(aggregated, grad_x, grad_w)


def solution(mesh):
    placed = (
        P(("row", "col"), None),
        P(),
        P("col", "row", None, None, None),
        P("col", "row", None),
        P("col", "row", None),
        P("col", "row"),
        P(("col", "row"), None),
    )
    return jax.shard_map(
        functools.partial(shards, mesh.shape["col"], mesh.shape["row"]),
        mesh=mesh,
        in_specs=placed,
        out_specs=(P(("col", "row"), None), P(("row", "col"), None), P()),
        check_vma=False,
    )
```

```python
import functools
import math

import jax
import jax.numpy as jnp
from jax import lax
from jax.experimental import pallas as pl
from jax.experimental.pallas import tpu as pltpu
from jax.sharding import PartitionSpec as P

BF16 = jnp.bfloat16
F32 = jnp.float32
MESH = pl.DeviceIdType.MESH


def each(count, body):
    if count <= 8:
        for step in range(count):
            body(step)
    else:
        lax.fori_loop(0, count, lambda step, _: (body(step), None)[1], None)


def matmul(a, b, contract=((1,), (0,))):
    return lax.dot_general(a, b, (contract, ((), ())), preferred_element_type=F32)


def layer_kernel(
    n_col, n_row, inner, near, pieces,
    rows_in, cols_in, count_in, feat_in, w_in, tiles_in, cot_ref,
    agg_ref, gx_ref, gw_ref,
    rows_ref, cols_ref, count_ref, feat_ref, w_ref, tiles_ref,
    feat_all, feat_t, ax_t, cot_all, pad, pad_t, a_ref, at_ref, w_hi, w_lo, proj, part, part_send, y_in, z_in,
    back, back_send, c_in, g_sum, g_part, g1_in, g1_sum, g2_in, gw_all,
    in_s, feat_s, feat_r, up_s, down_s, coty_s, cot_r, py_s, py_r, pz_s, pz_r, c_s, c_r,
    g1_s, g1_r, g2_s, g2_r, g3_s, g3_r, g4_s, g4_r, g5_s,
):
    outer = n_row // inner
    slots, tile = tiles_ref.shape[0], tiles_ref.shape[1]
    rows_dev, width = cot_ref.shape
    per_dev = rows_dev // tile
    dst_tiles, src_tiles = n_row * per_dev, n_col * per_dev
    col, row = lax.axis_index("col"), lax.axis_index("row")
    out_id, in_id = row // inner, row % inner
    g_rows = width // n_col
    g_piece = g_rows // pieces

    def send(src, dst, s_sem, r_sem, target):
        copy = pltpu.make_async_remote_copy(
            src_ref=src, dst_ref=dst, send_sem=s_sem, recv_sem=r_sem,
            device_id=target, device_id_type=MESH,
        )
        copy.start()

    def sent(ref, s_sem):
        pltpu.make_async_remote_copy(
            src_ref=ref, dst_ref=ref, send_sem=s_sem, recv_sem=s_sem,
            device_id={"col": col}, device_id_type=MESH,
        ).wait_send()

    def landed(ref, r_sem):
        pltpu.make_async_remote_copy(
            src_ref=ref, dst_ref=ref, send_sem=r_sem, recv_sem=r_sem,
            device_id={"col": col}, device_id_type=MESH,
        ).wait_recv()

    def col_at(d):
        return lax.rem(col + d, n_col)

    def row_at(d):
        return lax.rem(row + d, n_row)

    def out_at(d):
        return lax.rem(out_id + d, outer)

    def in_at(d):
        return lax.rem(in_id + d, inner)

    def reducer(r, body):
        if pieces == n_row:
            body()
        else:
            pl.when(r < pieces)(body)

    barrier = pltpu.get_barrier_semaphore()
    each(n_col - 1, lambda d: pl.semaphore_signal(
        barrier, inc=1, device_id={"col": col_at(d + 1)}, device_id_type=MESH))
    each(n_row - 1, lambda d: pl.semaphore_signal(
        barrier, inc=1, device_id={"row": row_at(d + 1)}, device_id_type=MESH))
    fetches = [
        pltpu.make_async_copy(source, target, in_s.at[k])
        for k, (source, target) in enumerate((
            (cot_ref, cot_all.at[row]), (feat_in, feat_ref), (tiles_in, tiles_ref),
            (rows_in, rows_ref), (cols_in, cols_ref), (count_in, count_ref), (w_in, w_ref),
        ))
    ]
    for fetch in fetches:
        fetch.start()
    fetches[1].wait()
    feat_all[col] = feat_ref[...].astype(BF16)
    fetches[0].wait()
    pl.semaphore_wait(barrier, n_col + n_row - 2)

    def chain(o, step, sems, d):
        slot = o * inner + in_id
        to = out_id + step
        send(cot_all.at[slot], cot_all.at[slot], sems.at[d], cot_r.at[slot], {"row": to * inner + in_id})

    def cot_forward(o, d_out):
        def one(d):
            slot = o * inner + in_id
            send(cot_all.at[slot], cot_all.at[slot], coty_s.at[d_out, d], cot_r.at[slot],
                 {"row": out_id * inner + in_at(d + 1)})
        each(inner - 1, one)

    if outer > 1:
        pl.when(out_id < outer - 1)(lambda: chain(out_id, 1, up_s, 0))
        pl.when(out_id > 0)(lambda: chain(out_id, -1, down_s, 0))
    cot_forward(out_id, 0)

    def feat_out(d):
        send(feat_all.at[col], feat_all.at[col], feat_s.at[d], feat_r.at[col], {"col": col_at(d + 1)})

    each(n_col - 1, feat_out)

    def pass_on(d):
        def from_below():
            o = out_id - d
            landed(cot_all.at[o * inner + in_id], cot_r.at[o * inner + in_id])
            pl.when(out_id < outer - 1)(lambda: chain(o, 1, up_s, d))
            cot_forward(o, o + 1)

        def from_above():
            o = out_id + d
            landed(cot_all.at[o * inner + in_id], cot_r.at[o * inner + in_id])
            pl.when(out_id > 0)(lambda: chain(o, -1, down_s, d))
            cot_forward(o, o + 1)

        pl.when(out_id - d >= 0)(from_below)
        pl.when(out_id + d < outer)(from_above)

    def pad_one(t):
        one = tiles_ref[t]
        pad[t] = one
        pad_t[t] = one.T

    for fetch in fetches[2:]:
        fetch.wait()
    each(slots, pad_one)
    pad[slots] = jnp.zeros((tile, tile), BF16)
    pad_t[slots] = jnp.zeros((tile, tile), BF16)
    live = count_ref[0, 0]
    places = [
        jnp.where(t < live, rows_ref[0, 0, t] * src_tiles + cols_ref[0, 0, t], -1) for t in range(slots)
    ]

    def lay(i):
        for k in range(src_tiles):
            index = jnp.int32(slots)
            for t in range(slots):
                index = jnp.where(places[t] == i * src_tiles + k, t, index)
            at = i * tile if isinstance(i, int) else pl.multiple_of(i * tile, tile)
            a_ref[pl.ds(at, tile), k * tile:(k + 1) * tile] = pad[index]
            at_ref[k * tile:(k + 1) * tile, pl.ds(at, tile)] = pad_t[index]

    half = dst_tiles // 2
    each(half, lay)
    if outer > 1:
        pass_on(1)
    each(dst_tiles - half, lambda i: lay(i + half))
    weight = w_ref[...]
    w_hi[...] = weight.astype(BF16)
    w_lo[...] = (weight - w_hi[...].astype(F32)).astype(BF16)

    def project(d):
        c = col_at(d)
        if not (isinstance(d, int) and d == 0):
            landed(feat_all.at[c], feat_r.at[c])
        block = feat_all[c]
        at = pl.multiple_of(c * rows_dev, rows_dev)
        proj[pl.ds(at, rows_dev), :] = (
            matmul(block, w_hi[...]) + matmul(block, w_lo[...])
        ).astype(BF16)
        feat_t[:, pl.ds(at, rows_dev)] = block.T

    project(0)

    span = inner * rows_dev

    def forward(o):
        at = o * span if isinstance(o, int) else pl.multiple_of(o * span, span)
        result = matmul(a_ref[pl.ds(at, span), :], proj[...]).reshape(inner, rows_dev, width)
        part[o] = result
        part_send[o] = result.astype(BF16)

    def weight_term(k, _):
        o = out_id + jnp.where(k % 2 == 1, -((k + 1) // 2), k // 2)

        def add():
            def one(e):
                slot = o * inner + in_at(e + 1)
                landed(cot_all.at[slot], cot_r.at[slot])
            each(inner - 1, one)
            block = ax_t[:, pl.ds(pl.multiple_of(o * span, span), span)]
            g_sum[...] += matmul(block, cot_all[pl.ds(o * inner, inner)].reshape(span, width))

        pl.when((o >= 0) & (o < outer))(add)

    def inner_out(d):
        o = out_at(d + 1)

        def one(e):
            target = in_at(e + 1)
            send(part_send.at[o, target], y_in.at[o, in_id], py_s.at[o, e], py_r.at[o, in_id],
                 {"row": out_id * inner + target})
        each(inner - 1, one)

    each(n_col - 1, lambda d: project(d + 1))
    each(min(outer - 2, 1), lambda d: pass_on(2))
    lax.fori_loop(0, outer, lambda o, _: forward(o), None)
    each(outer - 3, lambda d: pass_on(d + 3))
    first = outer // 2
    each(first, inner_out)
    ax_t[...] = matmul(feat_t[...], at_ref[...]).astype(BF16)
    g_sum[...] = jnp.zeros_like(g_sum)
    lax.fori_loop(0, 2 * outer - 1, weight_term, None)
    g_part[...] = g_sum[...].astype(BF16).reshape(n_col, g_rows, width)

    def g1_out(d):
        c = col_at(d + 1)
        send(g_part.at[c], g1_in.at[col], g1_s.at[d], g1_r.at[col], {"col": c})

    each(n_col - 1, g1_out)
    each(outer - first, lambda d: inner_out(d + first))

    back[...] = matmul(at_ref[...], cot_all[...].reshape(n_row * rows_dev, width))
    back_send[...] = back[...].astype(BF16).reshape(n_col, rows_dev, width)

    def c_out(d):
        c = col_at(d + 1)
        send(back_send.at[c], c_in.at[col], c_s.at[d], c_r.at[col], {"col": c})

    def inner_sum(o):
        def one(e):
            source = in_at(e + 1)
            landed(y_in.at[o, source], py_r.at[o, source])
            part[o, in_id] += y_in[o, source].astype(F32)
        each(inner - 1, one)

    def outer_out(d):
        o = out_at(d + 1)
        inner_sum(o)
        part_send[o, in_id] = part[o, in_id].astype(BF16)
        send(part_send.at[o, in_id], z_in.at[out_id], pz_s.at[d], pz_r.at[out_id], {"row": o * inner + in_id})

    early = max(outer - 2, 0)
    each(min(early, 1), outer_out)

    gw_part = g_part[col].astype(F32)
    def g1_add(d, total):
        c = col_at(d + 1)
        landed(g1_in.at[c], g1_r.at[c])
        return total + g1_in[c].astype(F32)
    for d in range(n_col - 1):
        gw_part = g1_add(d, gw_part)
    g1_sum[...] = gw_part.astype(BF16).reshape(pieces, g_piece, width)

    def g2_out(d):
        r = row_at(d + 1)
        reducer(r, lambda: send(g1_sum.at[r], g2_in.at[row], g2_s.at[d], g2_r.at[row], {"row": r}))

    each(n_row - 1, g2_out)
    each(n_col - 1, c_out)

    rest = outer - 1 - min(early, 1)
    each(rest, lambda d: outer_out(d + outer - 1 - rest))
    inner_sum(out_id)

    def g2_sum():
        def g2_wait(d):
            r = row_at(d + 1)
            landed(g2_in.at[r], g2_r.at[r])
        each(n_row - 1, g2_wait)
        g2_in[row] = g1_sum[row]
        total = g2_in[0].astype(F32)
        for r in range(1, n_row):
            total = total + g2_in[r].astype(F32)
        gw_all[col, row] = total.astype(BF16)

        def g3_out(d):
            send(gw_all.at[col, row], gw_all.at[col, row], g3_s.at[d], g3_r.at[row], {"row": row_at(d + 1)})
        each(n_row - 1, g3_out)

    reducer(row, g2_sum)

    def outer_col(d):
        return lax.rem(col // near + d, n_col // near) * near + col % near

    def near_col(d):
        return col // near * near + lax.rem(col % near + d, near)

    def to_near(c, r, d):
        def one(e):
            send(gw_all.at[c, r], gw_all.at[c, r], g5_s.at[d, r, e], g4_r.at[c, r], {"col": near_col(e + 1)})
        each(near - 1, one)

    def piece_out(r):
        def one(d):
            send(gw_all.at[col, r], gw_all.at[col, r], g4_s.at[d, r], g4_r.at[col, r], {"col": outer_col(d + 1)})
        each(n_col // near - 1, one)
        to_near(col, r, 0)

    def g3_wait(d):
        r = row_at(d + 1)

        def piece():
            landed(gw_all.at[col, r], g3_r.at[r])
            piece_out(r)
        reducer(r, piece)

    reducer(row, lambda: piece_out(row))
    each(n_row - 1, g3_wait)

    def c_add(d):
        c = col_at(d + 1)
        landed(c_in.at[c], c_r.at[c])
    each(n_col - 1, c_add)
    grad_y = back[pl.ds(pl.multiple_of(col * rows_dev, rows_dev), rows_dev), :]
    for d in range(n_col - 1):
        grad_y = grad_y + c_in[col_at(d + 1)].astype(F32)
    grad_y = grad_y.astype(BF16)
    gx_ref[...] = matmul(grad_y, w_hi[...], ((1,), (1,))) + matmul(grad_y, w_lo[...], ((1,), (1,)))

    def pass_piece(d):
        c = outer_col(d + 1)

        def one(e):
            r = row_at(e)

            def piece():
                landed(gw_all.at[c, r], g4_r.at[c, r])
                to_near(c, r, d + 1)
            reducer(r, piece)
        each(n_row, one)

    each(n_col // near - 1, pass_piece)

    def z_wait(d):
        o = out_at(d + 1)
        landed(z_in.at[o], pz_r.at[o])
        part[out_id, in_id] += z_in[o].astype(F32)

    each(outer - 1, z_wait)
    agg_ref[...] = part[out_id, in_id].astype(BF16)

    def last_wait(d):
        def one(e):
            c = near_col(e + 1)
            c = lax.rem(c // near + d, n_col // near) * near + c % near
            each(pieces, lambda r: landed(gw_all.at[c, r], g4_r.at[c, r]))
        each(near - 1, one)

    each(n_col // near, last_wait)
    gw_ref[...] = gw_all[...].reshape(width, width)

    each(n_col - 1, lambda d: sent(feat_all.at[0], feat_s.at[d]))
    def chain_sent(d):
        def up():
            sent(cot_ref, up_s.at[d])

        def down():
            sent(cot_ref, down_s.at[d])
        pl.when((out_id - d >= 0) & (out_id < outer - 1))(up)
        pl.when((out_id + d < outer) & (out_id > 0))(down)

    if outer > 1:
        each(outer, chain_sent)
    each(outer, lambda o: each(inner - 1, lambda e: sent(
        cot_ref, coty_s.at[jnp.where(out_id == o, 0, o + 1), e])))
    each(outer, lambda d: each(inner - 1, lambda e: sent(y_in.at[0, 0], py_s.at[d, e])))
    each(outer - 1, lambda d: sent(z_in.at[0], pz_s.at[d]))
    each(n_col - 1, lambda d: sent(c_in.at[0], c_s.at[d]))
    each(n_col - 1, lambda d: sent(g1_in.at[0], g1_s.at[d]))
    each(n_row - 1, lambda d: reducer(row_at(d + 1), lambda: sent(g2_in.at[0], g2_s.at[d])))
    reducer(row, lambda: each(n_row - 1, lambda d: sent(g2_in.at[0], g3_s.at[d])))
    each(pieces, lambda r: each(n_col // near - 1, lambda d: sent(g2_in.at[0], g4_s.at[d, r])))
    each(pieces, lambda r: each(n_col // near, lambda d: each(
        near - 1, lambda e: sent(g2_in.at[0], g5_s.at[d, r, e]))))


def write_kernel(agg_ref, gx_ref, gw_ref, agg_out, gx_out, gw_out, agg, gx, narrow, wide, sems):
    loads = [
        pltpu.make_async_copy(source, target, sems.at[k])
        for k, (source, target) in enumerate(((gw_ref, narrow), (agg_ref, agg), (gx_ref, gx)))
    ]
    stores = [
        pltpu.make_async_copy(source, target, sems.at[3 + k])
        for k, (source, target) in enumerate(((wide, gw_out), (agg, agg_out), (gx, gx_out)))
    ]
    for load in loads:
        load.start()
    for k in (1, 2):
        loads[k].wait()
        stores[k].start()
    loads[0].wait()
    wide[...] = narrow[...].astype(F32)
    for k in (0, 1, 2):
        if k == 0:
            stores[k].start()
        stores[k].wait()


def shards(n_col, n_row, features, weight, tiles, tile_rows, tile_cols, tile_count, cotangent):
    slots, tile = tiles.shape[2], tiles.shape[-1]
    rows_dev, width = features.shape
    inner = 2 if n_row % 2 == 0 else 1
    near = 2 if n_col % 2 == 0 else 1
    outer = n_row // inner
    g_rows = width // n_col
    pieces = min(n_row, g_rows // 16)
    g_piece = g_rows // pieces
    src, dst = n_col * rows_dev, n_row * rows_dev
    dma = pltpu.SemaphoreType.DMA
    vmem = pl.BlockSpec(memory_space=pltpu.VMEM)
    hbm = pl.BlockSpec(memory_space=pltpu.HBM)
    anywhere = pl.BlockSpec(memory_space=pl.ANY)
    buffers = [
        (features.shape, F32),
        (weight.shape, F32),
        (tiles.shape[2:], BF16),
        ((n_col, rows_dev, width), BF16),
        ((width, src), BF16),
        ((width, dst), BF16),
        ((n_row, rows_dev, width), BF16),
        ((slots + 1, tile, tile), BF16),
        ((slots + 1, tile, tile), BF16),
        ((dst, src), BF16),
        ((src, dst), BF16),
        ((width, width), BF16),
        ((width, width), BF16),
        ((src, width), BF16),
        ((outer, inner, rows_dev, width), F32),
        ((outer, inner, rows_dev, width), BF16),
        ((outer, inner, rows_dev, width), BF16),
        ((outer, rows_dev, width), BF16),
        ((src, width), F32),
        ((n_col, rows_dev, width), BF16),
        ((n_col, rows_dev, width), BF16),
        ((width, width), F32),
        ((n_col, g_rows, width), BF16),
        ((n_col, g_rows, width), BF16),
        ((pieces, g_piece, width), BF16),
        ((n_row, g_piece, width), BF16),
        ((n_col, pieces, g_piece, width), BF16),
    ]
    held = sum(math.prod(shape) * jnp.dtype(kind).itemsize for shape, kind in buffers)
    limit = max(56 * 2**20, min(held + 12 * 2**20, 63 * 2**20))
    sems = [
        (7,), (n_col,), (n_col,), (outer,), (outer,), (outer + 1, inner), (n_row,), (outer, inner), (outer, inner),
        (outer,), (outer,), (n_col,), (n_col,), (n_col,), (n_col,), (n_row,), (n_row,),
        (n_row,), (n_row,), (n_col, pieces), (n_col, pieces), (n_col, pieces, near),
    ]
    aggregated, grad_x, grad_w = pl.pallas_call(
        functools.partial(layer_kernel, n_col, n_row, inner, near, pieces),
        out_shape=(
            jax.ShapeDtypeStruct((rows_dev, width), BF16),
            jax.ShapeDtypeStruct((rows_dev, width), F32),
            jax.ShapeDtypeStruct((width, width), BF16),
        ),
        in_specs=[hbm] * 7,
        out_specs=(vmem, vmem, vmem),
        scratch_shapes=[pltpu.SMEM(one.shape, jnp.int32) for one in (tile_rows, tile_cols, tile_count)]
        + [pltpu.VMEM(shape, kind) for shape, kind in buffers] + [dma(s) for s in sems],
        compiler_params=pltpu.CompilerParams(
            collective_id=0, has_side_effects=True, vmem_limit_bytes=limit
        ),
        name="layer",
    )(
        tile_rows, tile_cols, tile_count,
        features, weight, tiles[0, 0], cotangent,
    )
    return pl.pallas_call(
        write_kernel,
        out_shape=(
            jax.ShapeDtypeStruct((rows_dev, width), BF16),
            jax.ShapeDtypeStruct((rows_dev, width), F32),
            jax.ShapeDtypeStruct((width, width), F32),
        ),
        in_specs=[anywhere] * 3,
        out_specs=(hbm,) * 3,
        scratch_shapes=[
            pltpu.VMEM((rows_dev, width), BF16), pltpu.VMEM((rows_dev, width), F32),
            pltpu.VMEM((width, width), BF16), pltpu.VMEM((width, width), F32), dma((6,)),
        ],
        compiler_params=pltpu.CompilerParams(vmem_limit_bytes=limit),
        name="write",
    )(aggregated, grad_x, grad_w)


def solution(mesh):
    placed = (
        P(("row", "col"), None),
        P(),
        P("col", "row", None, None, None),
        P("col", "row", None),
        P("col", "row", None),
        P("col", "row"),
        P(("col", "row"), None),
    )
    return jax.shard_map(
        functools.partial(shards, mesh.shape["col"], mesh.shape["row"]),
        mesh=mesh,
        in_specs=placed,
        out_specs=(P(("col", "row"), None), P(("row", "col"), None), P()),
        check_vma=False,
    )
```

```python
import functools
import math

import jax
import jax.numpy as jnp
from jax import lax
from jax.experimental import pallas as pl
from jax.experimental.pallas import tpu as pltpu
from jax.sharding import PartitionSpec as P

BF16 = jnp.bfloat16
F32 = jnp.float32
MESH = pl.DeviceIdType.MESH


def each(count, body):
    if count <= 8:
        for step in range(count):
            body(step)
    else:
        lax.fori_loop(0, count, lambda step, _: (body(step), None)[1], None)


def matmul(a, b, contract=((1,), (0,))):
    return lax.dot_general(a, b, (contract, ((), ())), preferred_element_type=F32)


def layer_kernel(
    n_col, n_row, inner, near, pieces,
    rows_in, cols_in, count_in, feat_in, w_in, tiles_in, cot_ref,
    agg_ref, gx_ref, gw_ref,
    rows_ref, cols_ref, count_ref, rows_v, cols_v, count_v, feat_ref, w_ref, tiles_all,
    feat_all, feat_t, ax_t, cot_all, pad, pad_t, a_ref, at_ref, w_hi, w_lo, proj, part, part_send, z_in,
    back, back_send, n1_in, n1_sum, n2_in, n2_sum, n3_in, g_sum, g_part, g1_in, g1_sum, g2_in, gw_all,
    in_s, move_s, y_s, y_r, fx_s, fn_s, ff_s, feat_r, up_s, down_s, cot_r, pz_s, pz_r,
    n1_s, n1_r, n2_s, n2_r, n3_s, n3_r, g1_s, g1_r, g2_s, g2_r, g3_s, g3_r, g4_s, g4_r, g5_s,
):
    outer = n_row // inner
    slots, tile = tiles_all.shape[1], tiles_all.shape[2]
    rows_dev, width = cot_ref.shape
    per_dev = rows_dev // tile
    src_tiles = n_col * per_dev
    wide = n_col // near
    col, row = lax.axis_index("col"), lax.axis_index("row")
    out_id, in_id = row // inner, row % inner
    wide_id, near_id = col // near, col % near
    g_rows = width // n_col
    g_piece = g_rows // pieces

    def send(src, dst, s_sem, r_sem, target):
        copy = pltpu.make_async_remote_copy(
            src_ref=src, dst_ref=dst, send_sem=s_sem, recv_sem=r_sem,
            device_id=target, device_id_type=MESH,
        )
        copy.start()

    def sent(ref, s_sem):
        pltpu.make_async_remote_copy(
            src_ref=ref, dst_ref=ref, send_sem=s_sem, recv_sem=s_sem,
            device_id={"col": col}, device_id_type=MESH,
        ).wait_send()

    def landed(ref, r_sem):
        pltpu.make_async_remote_copy(
            src_ref=ref, dst_ref=ref, send_sem=r_sem, recv_sem=r_sem,
            device_id={"col": col}, device_id_type=MESH,
        ).wait_recv()

    def col_at(d):
        return lax.rem(col + d, n_col)

    def row_at(d):
        return lax.rem(row + d, n_row)

    def out_at(d):
        return lax.rem(out_id + d, outer)

    def in_at(d):
        return lax.rem(in_id + d, inner)

    def outer_col(d):
        return lax.rem(wide_id + d, wide) * near + near_id

    def near_col(d):
        return wide_id * near + lax.rem(near_id + d, near)

    def place(j, c):
        return ((c % near) * inner + j) * wide + c // near

    def reducer(r, body):
        if pieces == n_row:
            body()
        else:
            pl.when(r < pieces)(body)

    barrier = pltpu.get_barrier_semaphore()
    each(n_col - 1, lambda d: pl.semaphore_signal(
        barrier, inc=1, device_id={"col": col_at(d + 1)}, device_id_type=MESH))
    each(n_row - 1, lambda d: pl.semaphore_signal(
        barrier, inc=1, device_id={"row": row_at(d + 1)}, device_id_type=MESH))
    index_pairs = ((rows_in, rows_v, rows_ref), (cols_in, cols_v, cols_ref), (count_in, count_v, count_ref))
    fetches = [
        pltpu.make_async_copy(source, target, in_s.at[k])
        for k, (source, target) in enumerate((
            (cot_ref, cot_all.at[out_id]), (feat_in, feat_ref), (tiles_in, tiles_all.at[in_id]),
            (rows_in, rows_v.at[in_id]), (cols_in, cols_v.at[in_id]), (count_in, count_v.at[in_id]),
            (w_in, w_ref),
        ))
    ]
    for fetch in fetches:
        fetch.start()
    own = place(in_id, col)
    fetches[1].wait()
    feat_all[own] = feat_ref[...].astype(BF16)
    fetches[0].wait()
    pl.semaphore_wait(barrier, n_col + n_row - 2)

    def chain(o, step, sems, d):
        send(cot_all.at[o], cot_all.at[o], sems.at[d], cot_r.at[o], {"row": (out_id + step) * inner + in_id})

    if outer > 1:
        pl.when(out_id < outer - 1)(lambda: chain(out_id, 1, up_s, 0))
        pl.when(out_id > 0)(lambda: chain(out_id, -1, down_s, 0))

    def swap(d):
        to = {"row": out_id * inner + in_at(d + 1)}
        send(feat_all.at[own], feat_all.at[own], y_s.at[0, d], feat_r.at[own], to)
        for k, (source, landing, _) in enumerate(index_pairs):
            send(source, landing.at[in_id], y_s.at[k + 1, d], y_r.at[k, in_id], to)
        send(tiles_in, tiles_all.at[in_id], y_s.at[4, d], y_r.at[3, in_id], to)

    each(inner - 1, swap)

    def feat_out(j, e):
        at = place(j, col)
        each(wide - 1, lambda d: send(
            feat_all.at[at], feat_all.at[at], fx_s.at[e, d], feat_r.at[at], {"col": outer_col(d + 1)}))
        each(near - 1, lambda d: send(
            feat_all.at[at], feat_all.at[at], fn_s.at[e, d], feat_r.at[at], {"col": near_col(d + 1)}))

    feat_out(in_id, 0)
    fetches[6].wait()
    weight = w_ref[...]
    w_hi[...] = weight.astype(BF16)
    w_lo[...] = (weight - w_hi[...].astype(F32)).astype(BF16)

    def pass_on(d):
        def from_below():
            o = out_id - d
            landed(cot_all.at[o], cot_r.at[o])
            pl.when(out_id < outer - 1)(lambda: chain(o, 1, up_s, d))

        def from_above():
            o = out_id + d
            landed(cot_all.at[o], cot_r.at[o])
            pl.when(out_id > 0)(lambda: chain(o, -1, down_s, d))

        pl.when(out_id - d >= 0)(from_below)
        pl.when(out_id + d < outer)(from_above)

    def feat_near(j, e):
        def one(d):
            at = place(j, outer_col(d + 1))
            landed(feat_all.at[at], feat_r.at[at])
            each(near - 1, lambda f: send(
                feat_all.at[at], feat_all.at[at], ff_s.at[e, d, f], feat_r.at[at], {"col": near_col(f + 1)}))
        each(wide - 1, one)

    def feat_in_on(e):
        j = in_at(e + 1)
        landed(feat_all.at[place(j, col)], feat_r.at[place(j, col)])
        feat_out(j, e + 1)

    each(inner - 1, feat_in_on)
    if outer > 1:
        pass_on(1)
    feat_near(in_id, 0)

    for fetch in fetches[2:6]:
        fetch.wait()

    def tiles_landed(e):
        j = in_at(e + 1)
        for k, (_, landing, _) in enumerate(index_pairs):
            landed(landing.at[j], y_r.at[k, j])
        landed(tiles_all.at[j], y_r.at[3, j])

    each(inner - 1, tiles_landed)
    moves = [pltpu.make_async_copy(landing, ref, move_s.at[k]) for k, (_, landing, ref) in enumerate(index_pairs)]
    for move in moves:
        move.start()

    def pad_one(t):
        for j in range(inner):
            one = tiles_all[j, t]
            pad[j, t] = one
            pad_t[j, t] = one.T

    each(slots, pad_one)
    for j in range(inner):
        pad[j, slots] = jnp.zeros((tile, tile), BF16)
        pad_t[j, slots] = jnp.zeros((tile, tile), BF16)
    for move in moves:
        move.wait()
    places = [
        [jnp.where(t < count_ref[j, 0, 0], rows_ref[j, 0, 0, t] * src_tiles + cols_ref[j, 0, 0, t], -1)
         for t in range(slots)] for j in range(inner)
    ]

    def lay(o):
        at = o * tile if isinstance(o, int) else pl.multiple_of(o * tile, tile)
        for j in range(inner):
            for k in range(src_tiles):
                index = jnp.int32(slots)
                for t in range(slots):
                    index = jnp.where(places[j][t] == (o * inner + in_id) * src_tiles + k, t, index)
                p = place(j, k)
                a_ref[pl.ds(at, tile), p * tile:(p + 1) * tile] = pad[j, index]
                at_ref[p * tile:(p + 1) * tile, pl.ds(at, tile)] = pad_t[j, index]

    each(outer, lay)
    each(min(outer - 2, 1), lambda d: pass_on(2))
    each(inner - 1, lambda e: feat_near(in_at(e + 1), e + 1))

    def near_landed(j, d):
        def one(e):
            c = lax.rem(wide_id + d, wide) * near + lax.rem(near_id + e + 1, near)
            landed(feat_all.at[place(j, c)], feat_r.at[place(j, c)])
        each(near - 1, one)

    for j in range(inner):
        each(wide, lambda d: near_landed(j, d))

    def project(p, _):
        at = pl.multiple_of(p * rows_dev, rows_dev)
        block = feat_all[p]
        proj[pl.ds(at, rows_dev), :] = (matmul(block, w_hi[...]) + matmul(block, w_lo[...])).astype(BF16)
        feat_t[:, pl.ds(at, rows_dev)] = block.T

    lax.fori_loop(0, inner * n_col, project, None)
    each(outer - 3, lambda d: pass_on(d + 3))

    def forward(d):
        o = out_at(d + 1)
        result = matmul(a_ref[pl.ds(pl.multiple_of(o * tile, tile), tile), :], proj[...])
        if isinstance(d, int) and d == outer - 1:
            part[...] = result
        else:
            part_send[o] = result.astype(BF16)
            send(part_send.at[o], z_in.at[out_id], pz_s.at[d], pz_r.at[out_id], {"row": o * inner + in_id})

    each(outer - 1, forward)
    part[...] = matmul(a_ref[pl.ds(pl.multiple_of(out_id * tile, tile), tile), :], proj[...])

    ax_t[...] = matmul(feat_t[...], at_ref[...]).astype(BF16)
    g_sum[...] = matmul(ax_t[...], cot_all[...].reshape(outer * rows_dev, width))
    g_part[...] = g_sum[...].astype(BF16).reshape(n_col, g_rows, width)

    def g1_out(d):
        c = col_at(d + 1)
        send(g_part.at[c], g1_in.at[col], g1_s.at[d], g1_r.at[col], {"col": c})

    each(n_col - 1, g1_out)

    back[...] = matmul(at_ref[...], cot_all[...].reshape(outer * rows_dev, width)).reshape(back.shape)
    back_send[...] = back[...].astype(BF16)

    def n1_out(d):
        e = lax.rem(near_id + d + 1, near)
        send(back_send.at[e], n1_in.at[near_id], n1_s.at[d], n1_r.at[near_id], {"col": near_col(d + 1)})

    each(near - 1, n1_out)

    def n1_add(d):
        e = lax.rem(near_id + d + 1, near)
        landed(n1_in.at[e], n1_r.at[e])
        back[near_id] += n1_in[e].astype(F32)

    each(near - 1, n1_add)
    n1_sum[...] = back[near_id].astype(BF16)

    def n2_out(d):
        j = in_at(d + 1)
        send(n1_sum.at[j], n2_in.at[in_id], n2_s.at[d], n2_r.at[in_id], {"row": out_id * inner + j})

    each(inner - 1, n2_out)

    gw_part = g_part[col].astype(F32)
    def g1_add(d, total):
        c = col_at(d + 1)
        landed(g1_in.at[c], g1_r.at[c])
        return total + g1_in[c].astype(F32)
    for d in range(n_col - 1):
        gw_part = g1_add(d, gw_part)
    g1_sum[...] = gw_part.astype(BF16).reshape(pieces, g_piece, width)

    def g2_out(d):
        r = row_at(d + 1)
        reducer(r, lambda: send(g1_sum.at[r], g2_in.at[row], g2_s.at[d], g2_r.at[row], {"row": r}))

    each(n_row - 1, g2_out)

    def n2_add(d):
        j = in_at(d + 1)
        landed(n2_in.at[j], n2_r.at[j])
        back[near_id, in_id] += n2_in[j].astype(F32)

    each(inner - 1, n2_add)
    n2_sum[...] = back[near_id, in_id].astype(BF16)

    def n3_out(d):
        w = lax.rem(wide_id + d + 1, wide)
        send(n2_sum.at[w], n3_in.at[wide_id], n3_s.at[d], n3_r.at[wide_id], {"col": outer_col(d + 1)})

    each(wide - 1, n3_out)

    def g2_sum():
        def g2_wait(d):
            r = row_at(d + 1)
            landed(g2_in.at[r], g2_r.at[r])
        each(n_row - 1, g2_wait)
        g2_in[row] = g1_sum[row]
        total = g2_in[0].astype(F32)
        for r in range(1, n_row):
            total = total + g2_in[r].astype(F32)
        gw_all[col, row] = total.astype(BF16)

        def g3_out(d):
            send(gw_all.at[col, row], gw_all.at[col, row], g3_s.at[d], g3_r.at[row], {"row": row_at(d + 1)})
        each(n_row - 1, g3_out)

    reducer(row, g2_sum)

    def to_near(c, r, d):
        def one(e):
            send(gw_all.at[c, r], gw_all.at[c, r], g5_s.at[d, r, e], g4_r.at[c, r], {"col": near_col(e + 1)})
        each(near - 1, one)

    def piece_out(r):
        def one(d):
            send(gw_all.at[col, r], gw_all.at[col, r], g4_s.at[d, r], g4_r.at[col, r], {"col": outer_col(d + 1)})
        each(n_col // near - 1, one)
        to_near(col, r, 0)

    def g3_wait(d):
        r = row_at(d + 1)

        def piece():
            landed(gw_all.at[col, r], g3_r.at[r])
            piece_out(r)
        reducer(r, piece)

    reducer(row, lambda: piece_out(row))
    each(n_row - 1, g3_wait)

    def n3_add(d):
        w = lax.rem(wide_id + d + 1, wide)
        landed(n3_in.at[w], n3_r.at[w])
        back[near_id, in_id, wide_id] += n3_in[w].astype(F32)

    each(wide - 1, n3_add)
    grad_y = back[near_id, in_id, wide_id]
    grad_y = grad_y.astype(BF16)
    gx_ref[...] = matmul(grad_y, w_hi[...], ((1,), (1,))) + matmul(grad_y, w_lo[...], ((1,), (1,)))

    def pass_piece(d):
        c = outer_col(d + 1)

        def one(e):
            r = row_at(e)

            def piece():
                landed(gw_all.at[c, r], g4_r.at[c, r])
                to_near(c, r, d + 1)
            reducer(r, piece)
        each(n_row, one)

    each(n_col // near - 1, pass_piece)

    def z_wait(d):
        o = out_at(d + 1)
        landed(z_in.at[o], pz_r.at[o])
        part[...] += z_in[o].astype(F32)

    each(outer - 1, z_wait)
    agg_ref[...] = part[...].astype(BF16)

    def last_wait(d):
        def one(e):
            c = near_col(e + 1)
            c = lax.rem(c // near + d, n_col // near) * near + c % near
            each(pieces, lambda r: landed(gw_all.at[c, r], g4_r.at[c, r]))
        each(near - 1, one)

    each(n_col // near, last_wait)
    gw_ref[...] = gw_all[...].reshape(width, width)

    def swap_sent(d):
        sent(feat_all.at[0], y_s.at[0, d])
        for k, (source, _, _) in enumerate(index_pairs):
            sent(source, y_s.at[k + 1, d])
        sent(tiles_in, y_s.at[4, d])

    each(inner - 1, swap_sent)
    for j in range(inner):
        each(wide - 1, lambda d: sent(feat_all.at[0], fx_s.at[j, d]))
        each(near - 1, lambda d: sent(feat_all.at[0], fn_s.at[j, d]))
        each(wide - 1, lambda d: each(near - 1, lambda f: sent(feat_all.at[0], ff_s.at[j, d, f])))

    def chain_sent(d):
        def up():
            sent(cot_ref, up_s.at[d])

        def down():
            sent(cot_ref, down_s.at[d])
        pl.when((out_id - d >= 0) & (out_id < outer - 1))(up)
        pl.when((out_id + d < outer) & (out_id > 0))(down)

    if outer > 1:
        each(outer, chain_sent)
    each(outer - 1, lambda d: sent(z_in.at[0], pz_s.at[d]))
    each(near - 1, lambda d: sent(n1_in.at[0], n1_s.at[d]))
    each(inner - 1, lambda d: sent(n2_in.at[0], n2_s.at[d]))
    each(wide - 1, lambda d: sent(n3_in.at[0], n3_s.at[d]))
    each(n_col - 1, lambda d: sent(g1_in.at[0], g1_s.at[d]))
    each(n_row - 1, lambda d: reducer(row_at(d + 1), lambda: sent(g2_in.at[0], g2_s.at[d])))
    reducer(row, lambda: each(n_row - 1, lambda d: sent(g2_in.at[0], g3_s.at[d])))
    each(pieces, lambda r: each(n_col // near - 1, lambda d: sent(g2_in.at[0], g4_s.at[d, r])))
    each(pieces, lambda r: each(n_col // near, lambda d: each(
        near - 1, lambda e: sent(g2_in.at[0], g5_s.at[d, r, e]))))


def write_kernel(agg_ref, gx_ref, gw_ref, agg_out, gx_out, gw_out, agg, gx, narrow, wide, sems):
    loads = [
        pltpu.make_async_copy(source, target, sems.at[k])
        for k, (source, target) in enumerate(((gw_ref, narrow), (agg_ref, agg), (gx_ref, gx)))
    ]
    stores = [
        pltpu.make_async_copy(source, target, sems.at[3 + k])
        for k, (source, target) in enumerate(((wide, gw_out), (agg, agg_out), (gx, gx_out)))
    ]
    for load in loads:
        load.start()
    for k in (1, 2):
        loads[k].wait()
        stores[k].start()
    loads[0].wait()
    wide[...] = narrow[...].astype(F32)
    for k in (0, 1, 2):
        if k == 0:
            stores[k].start()
        stores[k].wait()


def shards(n_col, n_row, features, weight, tiles, tile_rows, tile_cols, tile_count, cotangent):
    slots, tile = tiles.shape[2], tiles.shape[-1]
    rows_dev, width = features.shape
    inner = 2 if n_row % 2 == 0 else 1
    near = 2 if n_col % 2 == 0 else 1
    outer = n_row // inner
    g_rows = width // n_col
    pieces = min(n_row, g_rows // 16)
    g_piece = g_rows // pieces
    pair, half, wide = inner * n_col * rows_dev, outer * rows_dev, n_col // near
    dma = pltpu.SemaphoreType.DMA
    vmem = pl.BlockSpec(memory_space=pltpu.VMEM)
    hbm = pl.BlockSpec(memory_space=pltpu.HBM)
    anywhere = pl.BlockSpec(memory_space=pl.ANY)
    buffers = [
        (features.shape, F32),
        (weight.shape, F32),
        ((inner, *tiles.shape[2:]), BF16),
        ((inner * n_col, rows_dev, width), BF16),
        ((width, pair), BF16),
        ((width, half), BF16),
        ((outer, rows_dev, width), BF16),
        ((inner, slots + 1, tile, tile), BF16),
        ((inner, slots + 1, tile, tile), BF16),
        ((half, pair), BF16),
        ((pair, half), BF16),
        ((width, width), BF16),
        ((width, width), BF16),
        ((pair, width), BF16),
        ((rows_dev, width), F32),
        ((outer, rows_dev, width), BF16),
        ((outer, rows_dev, width), BF16),
        ((near, inner, wide, rows_dev, width), F32),
        ((near, inner, wide, rows_dev, width), BF16),
        ((near, inner, wide, rows_dev, width), BF16),
        ((inner, wide, rows_dev, width), BF16),
        ((inner, wide, rows_dev, width), BF16),
        ((wide, rows_dev, width), BF16),
        ((wide, rows_dev, width), BF16),
        ((width, width), F32),
        ((n_col, g_rows, width), BF16),
        ((n_col, g_rows, width), BF16),
        ((pieces, g_piece, width), BF16),
        ((n_row, g_piece, width), BF16),
        ((n_col, pieces, g_piece, width), BF16),
    ]
    held = sum(math.prod(shape) * jnp.dtype(kind).itemsize for shape, kind in buffers)
    limit = max(56 * 2**20, min(held + 12 * 2**20, 63 * 2**20))
    sems = [
        (7,), (3,), (5, inner), (4, inner), (inner, wide), (inner, near), (inner, wide, near),
        (inner * n_col,), (outer,), (outer,), (outer,), (outer,), (outer,),
        (near,), (near,), (inner,), (inner,), (wide,), (wide,), (n_col,), (n_col,), (n_row,), (n_row,),
        (n_row,), (n_row,), (n_col, pieces), (n_col, pieces), (n_col, pieces, near),
    ]
    aggregated, grad_x, grad_w = pl.pallas_call(
        functools.partial(layer_kernel, n_col, n_row, inner, near, pieces),
        out_shape=(
            jax.ShapeDtypeStruct((rows_dev, width), BF16),
            jax.ShapeDtypeStruct((rows_dev, width), F32),
            jax.ShapeDtypeStruct((width, width), BF16),
        ),
        in_specs=[hbm] * 7,
        out_specs=(vmem, vmem, vmem),
        scratch_shapes=[
            kind((inner, *one.shape), jnp.int32)
            for kind in (pltpu.SMEM, pltpu.VMEM) for one in (tile_rows, tile_cols, tile_count)
        ]
        + [pltpu.VMEM(shape, kind) for shape, kind in buffers] + [dma(s) for s in sems],
        compiler_params=pltpu.CompilerParams(
            collective_id=0, has_side_effects=True, vmem_limit_bytes=limit
        ),
        name="layer",
    )(
        tile_rows, tile_cols, tile_count,
        features, weight, tiles[0, 0], cotangent,
    )
    return pl.pallas_call(
        write_kernel,
        out_shape=(
            jax.ShapeDtypeStruct((rows_dev, width), BF16),
            jax.ShapeDtypeStruct((rows_dev, width), F32),
            jax.ShapeDtypeStruct((width, width), F32),
        ),
        in_specs=[anywhere] * 3,
        out_specs=(hbm,) * 3,
        scratch_shapes=[
            pltpu.VMEM((rows_dev, width), BF16), pltpu.VMEM((rows_dev, width), F32),
            pltpu.VMEM((width, width), BF16), pltpu.VMEM((width, width), F32), dma((6,)),
        ],
        compiler_params=pltpu.CompilerParams(vmem_limit_bytes=limit),
        name="write",
    )(aggregated, grad_x, grad_w)


def solution(mesh):
    placed = (
        P(("row", "col"), None),
        P(),
        P("col", "row", None, None, None),
        P("col", "row", None),
        P("col", "row", None),
        P("col", "row"),
        P(("col", "row"), None),
    )
    return jax.shard_map(
        functools.partial(shards, mesh.shape["col"], mesh.shape["row"]),
        mesh=mesh,
        in_specs=placed,
        out_specs=(P(("col", "row"), None), P(("row", "col"), None), P()),
        check_vma=False,
    )
```

```python
import functools
import math

import jax
import jax.numpy as jnp
from jax import lax
from jax.experimental import pallas as pl
from jax.experimental.pallas import tpu as pltpu
from jax.sharding import PartitionSpec as P

BF16 = jnp.bfloat16
F32 = jnp.float32
MESH = pl.DeviceIdType.MESH


def each(count, body):
    if count <= 8:
        for step in range(count):
            body(step)
    else:
        lax.fori_loop(0, count, lambda step, _: (body(step), None)[1], None)


def matmul(a, b, contract=((1,), (0,))):
    return lax.dot_general(a, b, (contract, ((), ())), preferred_element_type=F32)


def layer_kernel(
    n_col, n_row, inner, near, pieces,
    rows_in, cols_in, count_in, feat_in, w_in, tiles_in, cot_ref,
    agg_ref, gx_ref, gw_ref,
    rows_ref, cols_ref, count_ref, rows_v, cols_v, count_v, feat_ref, w_ref, tiles_all,
    feat_all, feat_t, ax_t, cot_all, pad, pad_t, a_ref, at_ref, w_hi, w_lo, proj, part, part_send, z_in,
    back, back_send, n1_in, n1_sum, n2_in, n2_sum, n3_in, g_part, g1_in, g1_sum, g2_in, gw_all,
    in_s, move_s, y_s, y_r, fx_s, fn_s, ff_s, feat_r, up_s, down_s, cot_r, pz_s, pz_r,
    n1_s, n1_r, n2_s, n2_r, n3_s, n3_r, g1_s, g1_r, g2_s, g2_r, g3_s, g3_r, g4_s, g4_r, g5_s,
):
    outer = n_row // inner
    slots, tile = tiles_all.shape[1], tiles_all.shape[2]
    rows_dev, width = cot_ref.shape
    per_dev = rows_dev // tile
    src_tiles = n_col * per_dev
    wide = n_col // near
    col, row = lax.axis_index("col"), lax.axis_index("row")
    out_id, in_id = row // inner, row % inner
    wide_id, near_id = col // near, col % near
    g_rows = width // n_col
    g_piece = g_rows // pieces

    def send(src, dst, s_sem, r_sem, target):
        copy = pltpu.make_async_remote_copy(
            src_ref=src, dst_ref=dst, send_sem=s_sem, recv_sem=r_sem,
            device_id=target, device_id_type=MESH,
        )
        copy.start()

    def sent(ref, s_sem):
        pltpu.make_async_remote_copy(
            src_ref=ref, dst_ref=ref, send_sem=s_sem, recv_sem=s_sem,
            device_id={"col": col}, device_id_type=MESH,
        ).wait_send()

    def landed(ref, r_sem):
        pltpu.make_async_remote_copy(
            src_ref=ref, dst_ref=ref, send_sem=r_sem, recv_sem=r_sem,
            device_id={"col": col}, device_id_type=MESH,
        ).wait_recv()

    def col_at(d):
        return lax.rem(col + d, n_col)

    def row_at(d):
        return lax.rem(row + d, n_row)

    def out_at(d):
        return lax.rem(out_id + d, outer)

    def in_at(d):
        return lax.rem(in_id + d, inner)

    def outer_col(d):
        return lax.rem(wide_id + d, wide) * near + near_id

    def near_col(d):
        return wide_id * near + lax.rem(near_id + d, near)

    def place(j, c):
        return ((c % near) * inner + j) * wide + c // near

    def reducer(r, body):
        if pieces == n_row:
            body()
        else:
            pl.when(r < pieces)(body)

    barrier = pltpu.get_barrier_semaphore()
    each(n_col - 1, lambda d: pl.semaphore_signal(
        barrier, inc=1, device_id={"col": col_at(d + 1)}, device_id_type=MESH))
    each(n_row - 1, lambda d: pl.semaphore_signal(
        barrier, inc=1, device_id={"row": row_at(d + 1)}, device_id_type=MESH))
    index_pairs = ((rows_in, rows_v, rows_ref), (cols_in, cols_v, cols_ref), (count_in, count_v, count_ref))
    fetches = [
        pltpu.make_async_copy(source, target, in_s.at[k])
        for k, (source, target) in enumerate((
            (cot_ref, cot_all.at[out_id]), (feat_in, feat_ref), (tiles_in, tiles_all.at[in_id]),
            (rows_in, rows_v.at[in_id]), (cols_in, cols_v.at[in_id]), (count_in, count_v.at[in_id]),
            (w_in, w_ref),
        ))
    ]
    for fetch in fetches:
        fetch.start()
    own = place(in_id, col)
    fetches[1].wait()
    feat_all[own] = feat_ref[...].astype(BF16)
    fetches[0].wait()
    pl.semaphore_wait(barrier, n_col + n_row - 2)

    def chain(o, step, sems, d):
        send(cot_all.at[o], cot_all.at[o], sems.at[d], cot_r.at[o], {"row": (out_id + step) * inner + in_id})

    if outer > 1:
        pl.when(out_id < outer - 1)(lambda: chain(out_id, 1, up_s, 0))
        pl.when(out_id > 0)(lambda: chain(out_id, -1, down_s, 0))

    def swap(d):
        to = {"row": out_id * inner + in_at(d + 1)}
        send(feat_all.at[own], feat_all.at[own], y_s.at[0, d], feat_r.at[own], to)
        for k, (source, landing, _) in enumerate(index_pairs):
            send(source, landing.at[in_id], y_s.at[k + 1, d], y_r.at[k, in_id], to)
        send(tiles_in, tiles_all.at[in_id], y_s.at[4, d], y_r.at[3, in_id], to)

    each(inner - 1, swap)

    def feat_out(j, e):
        at = place(j, col)
        each(wide - 1, lambda d: send(
            feat_all.at[at], feat_all.at[at], fx_s.at[e, d], feat_r.at[at], {"col": outer_col(d + 1)}))
        each(near - 1, lambda d: send(
            feat_all.at[at], feat_all.at[at], fn_s.at[e, d], feat_r.at[at], {"col": near_col(d + 1)}))

    feat_out(in_id, 0)
    fetches[6].wait()
    weight = w_ref[...]
    w_hi[...] = weight.astype(BF16)
    w_lo[...] = (weight - w_hi[...].astype(F32)).astype(BF16)

    def pass_on(d):
        def from_below():
            o = out_id - d
            landed(cot_all.at[o], cot_r.at[o])
            pl.when(out_id < outer - 1)(lambda: chain(o, 1, up_s, d))

        def from_above():
            o = out_id + d
            landed(cot_all.at[o], cot_r.at[o])
            pl.when(out_id > 0)(lambda: chain(o, -1, down_s, d))

        pl.when(out_id - d >= 0)(from_below)
        pl.when(out_id + d < outer)(from_above)

    def feat_near(j, e):
        def one(d):
            at = place(j, outer_col(d + 1))
            landed(feat_all.at[at], feat_r.at[at])
            each(near - 1, lambda f: send(
                feat_all.at[at], feat_all.at[at], ff_s.at[e, d, f], feat_r.at[at], {"col": near_col(f + 1)}))
        each(wide - 1, one)

    def feat_in_on(e):
        j = in_at(e + 1)
        landed(feat_all.at[place(j, col)], feat_r.at[place(j, col)])
        feat_out(j, e + 1)

    each(inner - 1, feat_in_on)
    if outer > 1:
        pass_on(1)
    feat_near(in_id, 0)

    for fetch in fetches[2:6]:
        fetch.wait()

    def tiles_landed(e):
        j = in_at(e + 1)
        for k, (_, landing, _) in enumerate(index_pairs):
            landed(landing.at[j], y_r.at[k, j])
        landed(tiles_all.at[j], y_r.at[3, j])

    each(inner - 1, tiles_landed)
    moves = [pltpu.make_async_copy(landing, ref, move_s.at[k]) for k, (_, landing, ref) in enumerate(index_pairs)]
    for move in moves:
        move.start()

    def pad_one(t):
        for j in range(inner):
            one = tiles_all[j, t]
            pad[j, t] = one
            pad_t[j, t] = one.T

    each(slots, pad_one)
    for j in range(inner):
        pad[j, slots] = jnp.zeros((tile, tile), BF16)
        pad_t[j, slots] = jnp.zeros((tile, tile), BF16)
    for move in moves:
        move.wait()
    places = [
        [jnp.where(t < count_ref[j, 0, 0], rows_ref[j, 0, 0, t] * src_tiles + cols_ref[j, 0, 0, t], -1)
         for t in range(slots)] for j in range(inner)
    ]

    def lay(o):
        at = o * tile if isinstance(o, int) else pl.multiple_of(o * tile, tile)
        for j in range(inner):
            for k in range(src_tiles):
                index = jnp.int32(slots)
                for t in range(slots):
                    index = jnp.where(places[j][t] == (o * inner + in_id) * src_tiles + k, t, index)
                p = place(j, k)
                a_ref[pl.ds(at, tile), p * tile:(p + 1) * tile] = pad[j, index]
                at_ref[p * tile:(p + 1) * tile, pl.ds(at, tile)] = pad_t[j, index]

    each(outer, lay)
    each(min(outer - 2, 1), lambda d: pass_on(2))

    def near_landed(j, d):
        def one(e):
            c = lax.rem(wide_id + d, wide) * near + lax.rem(near_id + e + 1, near)
            landed(feat_all.at[place(j, c)], feat_r.at[place(j, c)])
        each(near - 1, one)

    def project(j):
        def one(c, _):
            p = place(j, c)
            block = feat_all[p]
            proj[pl.ds(pl.multiple_of(p * rows_dev, rows_dev), rows_dev), :] = (
                matmul(block, w_hi[...]) + matmul(block, w_lo[...])
            ).astype(BF16)
        lax.fori_loop(0, n_col, one, None)

    def turn(j):
        def one(c, _):
            p = place(j, c)
            feat_t[:, pl.ds(pl.multiple_of(p * rows_dev, rows_dev), rows_dev)] = feat_all[p].T
        lax.fori_loop(0, n_col, one, None)

    each(wide, lambda d: near_landed(in_id, d))
    turn(in_id)
    project(in_id)
    each(inner - 1, lambda e: feat_near(in_at(e + 1), e + 1))
    for e in range(1, inner):
        each(wide, lambda d: near_landed(in_at(e), d))
        turn(in_at(e))

    ax_t[...] = matmul(feat_t[...], at_ref[...]).astype(BF16)
    each(outer - 3, lambda d: pass_on(d + 3))
    g_part[...] = matmul(
        ax_t[...], cot_all[...].reshape(outer * rows_dev, width)
    ).astype(BF16).reshape(n_col, g_rows, width)

    def g1_out(d):
        c = col_at(d + 1)
        send(g_part.at[c], g1_in.at[col], g1_s.at[d], g1_r.at[col], {"col": c})

    each(n_col - 1, g1_out)

    for e in range(1, inner):
        project(in_at(e))

    def forward(d):
        o = out_at(d + 1)
        part_send[o] = matmul(
            a_ref[pl.ds(pl.multiple_of(o * tile, tile), tile), :], proj[...]
        ).astype(BF16)
        send(part_send.at[o], z_in.at[out_id], pz_s.at[d], pz_r.at[out_id], {"row": o * inner + in_id})

    each(outer - 1, forward)
    part[...] = matmul(a_ref[pl.ds(pl.multiple_of(out_id * tile, tile), tile), :], proj[...])

    back[...] = matmul(at_ref[...], cot_all[...].reshape(outer * rows_dev, width)).reshape(back.shape)
    back_send[...] = back[...].astype(BF16)

    def n1_out(d):
        e = lax.rem(near_id + d + 1, near)
        send(back_send.at[e], n1_in.at[near_id], n1_s.at[d], n1_r.at[near_id], {"col": near_col(d + 1)})

    each(near - 1, n1_out)

    def n1_add(d):
        e = lax.rem(near_id + d + 1, near)
        landed(n1_in.at[e], n1_r.at[e])
        back[near_id] += n1_in[e].astype(F32)

    each(near - 1, n1_add)
    n1_sum[...] = back[near_id].astype(BF16)

    def n2_out(d):
        j = in_at(d + 1)
        send(n1_sum.at[j], n2_in.at[in_id], n2_s.at[d], n2_r.at[in_id], {"row": out_id * inner + j})

    each(inner - 1, n2_out)

    gw_part = g_part[col].astype(F32)
    def g1_add(d, total):
        c = col_at(d + 1)
        landed(g1_in.at[c], g1_r.at[c])
        return total + g1_in[c].astype(F32)
    for d in range(n_col - 1):
        gw_part = g1_add(d, gw_part)
    g1_sum[...] = gw_part.astype(BF16).reshape(pieces, g_piece, width)

    def g2_out(d):
        r = row_at(d + 1)
        reducer(r, lambda: send(g1_sum.at[r], g2_in.at[row], g2_s.at[d], g2_r.at[row], {"row": r}))

    each(n_row - 1, g2_out)

    def n2_add(d):
        j = in_at(d + 1)
        landed(n2_in.at[j], n2_r.at[j])
        back[near_id, in_id] += n2_in[j].astype(F32)

    each(inner - 1, n2_add)
    n2_sum[...] = back[near_id, in_id].astype(BF16)

    def n3_out(d):
        w = lax.rem(wide_id + d + 1, wide)
        send(n2_sum.at[w], n3_in.at[wide_id], n3_s.at[d], n3_r.at[wide_id], {"col": outer_col(d + 1)})

    each(wide - 1, n3_out)

    def g2_sum():
        def g2_wait(d):
            r = row_at(d + 1)
            landed(g2_in.at[r], g2_r.at[r])
        each(n_row - 1, g2_wait)
        g2_in[row] = g1_sum[row]
        total = g2_in[0].astype(F32)
        for r in range(1, n_row):
            total = total + g2_in[r].astype(F32)
        gw_all[col, row] = total.astype(BF16)

        def g3_out(d):
            send(gw_all.at[col, row], gw_all.at[col, row], g3_s.at[d], g3_r.at[row], {"row": row_at(d + 1)})
        each(n_row - 1, g3_out)

    reducer(row, g2_sum)

    def to_near(c, r, d):
        def one(e):
            send(gw_all.at[c, r], gw_all.at[c, r], g5_s.at[d, r, e], g4_r.at[c, r], {"col": near_col(e + 1)})
        each(near - 1, one)

    def piece_out(r):
        def one(d):
            send(gw_all.at[col, r], gw_all.at[col, r], g4_s.at[d, r], g4_r.at[col, r], {"col": outer_col(d + 1)})
        each(n_col // near - 1, one)
        to_near(col, r, 0)

    def g3_wait(d):
        r = row_at(d + 1)

        def piece():
            landed(gw_all.at[col, r], g3_r.at[r])
            piece_out(r)
        reducer(r, piece)

    reducer(row, lambda: piece_out(row))
    each(n_row - 1, g3_wait)

    def n3_add(d):
        w = lax.rem(wide_id + d + 1, wide)
        landed(n3_in.at[w], n3_r.at[w])
        back[near_id, in_id, wide_id] += n3_in[w].astype(F32)

    each(wide - 1, n3_add)
    grad_y = back[near_id, in_id, wide_id]
    grad_y = grad_y.astype(BF16)
    gx_ref[...] = matmul(grad_y, w_hi[...], ((1,), (1,))) + matmul(grad_y, w_lo[...], ((1,), (1,)))

    def pass_piece(d):
        c = outer_col(d + 1)

        def one(e):
            r = row_at(e)

            def piece():
                landed(gw_all.at[c, r], g4_r.at[c, r])
                to_near(c, r, d + 1)
            reducer(r, piece)
        each(n_row, one)

    each(n_col // near - 1, pass_piece)

    def z_wait(d):
        o = out_at(d + 1)
        landed(z_in.at[o], pz_r.at[o])
        part[...] += z_in[o].astype(F32)

    each(outer - 1, z_wait)
    agg_ref[...] = part[...].astype(BF16)

    def last_wait(d):
        def one(e):
            c = near_col(e + 1)
            c = lax.rem(c // near + d, n_col // near) * near + c % near
            each(pieces, lambda r: landed(gw_all.at[c, r], g4_r.at[c, r]))
        each(near - 1, one)

    each(n_col // near, last_wait)
    gw_ref[...] = gw_all[...].reshape(width, width)

    def swap_sent(d):
        sent(feat_all.at[0], y_s.at[0, d])
        for k, (source, _, _) in enumerate(index_pairs):
            sent(source, y_s.at[k + 1, d])
        sent(tiles_in, y_s.at[4, d])

    each(inner - 1, swap_sent)
    for j in range(inner):
        each(wide - 1, lambda d: sent(feat_all.at[0], fx_s.at[j, d]))
        each(near - 1, lambda d: sent(feat_all.at[0], fn_s.at[j, d]))
        each(wide - 1, lambda d: each(near - 1, lambda f: sent(feat_all.at[0], ff_s.at[j, d, f])))

    def chain_sent(d):
        def up():
            sent(cot_ref, up_s.at[d])

        def down():
            sent(cot_ref, down_s.at[d])
        pl.when((out_id - d >= 0) & (out_id < outer - 1))(up)
        pl.when((out_id + d < outer) & (out_id > 0))(down)

    if outer > 1:
        each(outer, chain_sent)
    each(outer - 1, lambda d: sent(z_in.at[0], pz_s.at[d]))
    each(near - 1, lambda d: sent(n1_in.at[0], n1_s.at[d]))
    each(inner - 1, lambda d: sent(n2_in.at[0], n2_s.at[d]))
    each(wide - 1, lambda d: sent(n3_in.at[0], n3_s.at[d]))
    each(n_col - 1, lambda d: sent(g1_in.at[0], g1_s.at[d]))
    each(n_row - 1, lambda d: reducer(row_at(d + 1), lambda: sent(g2_in.at[0], g2_s.at[d])))
    reducer(row, lambda: each(n_row - 1, lambda d: sent(g2_in.at[0], g3_s.at[d])))
    each(pieces, lambda r: each(n_col // near - 1, lambda d: sent(g2_in.at[0], g4_s.at[d, r])))
    each(pieces, lambda r: each(n_col // near, lambda d: each(
        near - 1, lambda e: sent(g2_in.at[0], g5_s.at[d, r, e]))))


def write_kernel(agg_ref, gx_ref, gw_ref, agg_out, gx_out, gw_out, agg, gx, narrow, wide, sems):
    loads = [
        pltpu.make_async_copy(source, target, sems.at[k])
        for k, (source, target) in enumerate(((gw_ref, narrow), (agg_ref, agg), (gx_ref, gx)))
    ]
    stores = [
        pltpu.make_async_copy(source, target, sems.at[3 + k])
        for k, (source, target) in enumerate(((wide, gw_out), (agg, agg_out), (gx, gx_out)))
    ]
    for load in loads:
        load.start()
    for k in (1, 2):
        loads[k].wait()
        stores[k].start()
    loads[0].wait()
    wide[...] = narrow[...].astype(F32)
    for k in (0, 1, 2):
        if k == 0:
            stores[k].start()
        stores[k].wait()


def shards(n_col, n_row, features, weight, tiles, tile_rows, tile_cols, tile_count, cotangent):
    slots, tile = tiles.shape[2], tiles.shape[-1]
    rows_dev, width = features.shape
    inner = 2 if n_row % 2 == 0 else 1
    near = 2 if n_col % 2 == 0 else 1
    outer = n_row // inner
    g_rows = width // n_col
    pieces = min(n_row, g_rows // 16)
    g_piece = g_rows // pieces
    pair, half, wide = inner * n_col * rows_dev, outer * rows_dev, n_col // near
    dma = pltpu.SemaphoreType.DMA
    vmem = pl.BlockSpec(memory_space=pltpu.VMEM)
    hbm = pl.BlockSpec(memory_space=pltpu.HBM)
    anywhere = pl.BlockSpec(memory_space=pl.ANY)
    buffers = [
        (features.shape, F32),
        (weight.shape, F32),
        ((inner, *tiles.shape[2:]), BF16),
        ((inner * n_col, rows_dev, width), BF16),
        ((width, pair), BF16),
        ((width, half), BF16),
        ((outer, rows_dev, width), BF16),
        ((inner, slots + 1, tile, tile), BF16),
        ((inner, slots + 1, tile, tile), BF16),
        ((half, pair), BF16),
        ((pair, half), BF16),
        ((width, width), BF16),
        ((width, width), BF16),
        ((pair, width), BF16),
        ((rows_dev, width), F32),
        ((outer, rows_dev, width), BF16),
        ((outer, rows_dev, width), BF16),
        ((near, inner, wide, rows_dev, width), F32),
        ((near, inner, wide, rows_dev, width), BF16),
        ((near, inner, wide, rows_dev, width), BF16),
        ((inner, wide, rows_dev, width), BF16),
        ((inner, wide, rows_dev, width), BF16),
        ((wide, rows_dev, width), BF16),
        ((wide, rows_dev, width), BF16),
        ((n_col, g_rows, width), BF16),
        ((n_col, g_rows, width), BF16),
        ((pieces, g_piece, width), BF16),
        ((n_row, g_piece, width), BF16),
        ((n_col, pieces, g_piece, width), BF16),
    ]
    held = sum(math.prod(shape) * jnp.dtype(kind).itemsize for shape, kind in buffers)
    limit = max(56 * 2**20, min(held + 12 * 2**20, 63 * 2**20))
    sems = [
        (7,), (3,), (5, inner), (4, inner), (inner, wide), (inner, near), (inner, wide, near),
        (inner * n_col,), (outer,), (outer,), (outer,), (outer,), (outer,),
        (near,), (near,), (inner,), (inner,), (wide,), (wide,), (n_col,), (n_col,), (n_row,), (n_row,),
        (n_row,), (n_row,), (n_col, pieces), (n_col, pieces), (n_col, pieces, near),
    ]
    aggregated, grad_x, grad_w = pl.pallas_call(
        functools.partial(layer_kernel, n_col, n_row, inner, near, pieces),
        out_shape=(
            jax.ShapeDtypeStruct((rows_dev, width), BF16),
            jax.ShapeDtypeStruct((rows_dev, width), F32),
            jax.ShapeDtypeStruct((width, width), BF16),
        ),
        in_specs=[hbm] * 7,
        out_specs=(vmem, vmem, vmem),
        scratch_shapes=[
            kind((inner, *one.shape), jnp.int32)
            for kind in (pltpu.SMEM, pltpu.VMEM) for one in (tile_rows, tile_cols, tile_count)
        ]
        + [pltpu.VMEM(shape, kind) for shape, kind in buffers] + [dma(s) for s in sems],
        compiler_params=pltpu.CompilerParams(
            collective_id=0, has_side_effects=True, vmem_limit_bytes=limit
        ),
        name="layer",
    )(
        tile_rows, tile_cols, tile_count,
        features, weight, tiles[0, 0], cotangent,
    )
    return pl.pallas_call(
        write_kernel,
        out_shape=(
            jax.ShapeDtypeStruct((rows_dev, width), BF16),
            jax.ShapeDtypeStruct((rows_dev, width), F32),
            jax.ShapeDtypeStruct((width, width), F32),
        ),
        in_specs=[anywhere] * 3,
        out_specs=(hbm,) * 3,
        scratch_shapes=[
            pltpu.VMEM((rows_dev, width), BF16), pltpu.VMEM((rows_dev, width), F32),
            pltpu.VMEM((width, width), BF16), pltpu.VMEM((width, width), F32), dma((6,)),
        ],
        compiler_params=pltpu.CompilerParams(vmem_limit_bytes=limit),
        name="write",
    )(aggregated, grad_x, grad_w)


def solution(mesh):
    placed = (
        P(("row", "col"), None),
        P(),
        P("col", "row", None, None, None),
        P("col", "row", None),
        P("col", "row", None),
        P("col", "row"),
        P(("col", "row"), None),
    )
    return jax.shard_map(
        functools.partial(shards, mesh.shape["col"], mesh.shape["row"]),
        mesh=mesh,
        in_specs=placed,
        out_specs=(P(("col", "row"), None), P(("row", "col"), None), P()),
        check_vma=False,
    )
```

```python
import functools
import math

import jax
import jax.numpy as jnp
from jax import lax
from jax.experimental import pallas as pl
from jax.experimental.pallas import tpu as pltpu
from jax.sharding import PartitionSpec as P

BF16 = jnp.bfloat16
F32 = jnp.float32
MESH = pl.DeviceIdType.MESH


def each(count, body):
    if count <= 8:
        for step in range(count):
            body(step)
    else:
        lax.fori_loop(0, count, lambda step, _: (body(step), None)[1], None)


def matmul(a, b, contract=((1,), (0,))):
    return lax.dot_general(a, b, (contract, ((), ())), preferred_element_type=F32)


def layer_kernel(
    n_col, n_row, inner, near, pieces,
    rows_in, cols_in, count_in, feat_in, w_in, tiles_in, cot_ref,
    agg_ref, gx_ref, gw_ref,
    rows_ref, cols_ref, count_ref, rows_v, cols_v, count_v, feat_ref, w_ref, tiles_all,
    feat_all, feat_t, ax_t, cot_all, pad, pad_t, a_ref, at_ref, w_hi, w_lo, proj, part, part_send, z_in,
    back, back_send, n1_in, n1_sum, n2_in, n2_sum, n3_in, g_part, g1_in, g1_sum, g2_in, gw_all,
    in_s, move_s, y_s, y_r, fx_s, fn_s, ff_s, feat_r, up_s, down_s, cot_r, pz_s, pz_r,
    n1_s, n1_r, n2_s, n2_r, n3_s, n3_r, g1_s, g1_r, g2_s, g2_r, g3_s, g3_r, g4_s, g4_r, g5_s,
):
    outer = n_row // inner
    slots, tile = tiles_all.shape[1], tiles_all.shape[2]
    rows_dev, width = cot_ref.shape
    per_dev = rows_dev // tile
    src_tiles = n_col * per_dev
    wide = n_col // near
    col, row = lax.axis_index("col"), lax.axis_index("row")
    out_id, in_id = row // inner, row % inner
    wide_id, near_id = col // near, col % near
    g_rows = width // n_col
    g_piece = g_rows // pieces

    def send(src, dst, s_sem, r_sem, target):
        copy = pltpu.make_async_remote_copy(
            src_ref=src, dst_ref=dst, send_sem=s_sem, recv_sem=r_sem,
            device_id=target, device_id_type=MESH,
        )
        copy.start()

    def sent(ref, s_sem):
        pltpu.make_async_remote_copy(
            src_ref=ref, dst_ref=ref, send_sem=s_sem, recv_sem=s_sem,
            device_id={"col": col}, device_id_type=MESH,
        ).wait_send()

    def landed(ref, r_sem):
        pltpu.make_async_remote_copy(
            src_ref=ref, dst_ref=ref, send_sem=r_sem, recv_sem=r_sem,
            device_id={"col": col}, device_id_type=MESH,
        ).wait_recv()

    def col_at(d):
        return lax.rem(col + d, n_col)

    def row_at(d):
        return lax.rem(row + d, n_row)

    def out_at(d):
        return lax.rem(out_id + d, outer)

    def in_at(d):
        return lax.rem(in_id + d, inner)

    def outer_col(d):
        return lax.rem(wide_id + d, wide) * near + near_id

    def near_col(d):
        return wide_id * near + lax.rem(near_id + d, near)

    def place(j, c):
        return ((c % near) * inner + j) * wide + c // near

    def reducer(r, body):
        if pieces == n_row:
            body()
        else:
            pl.when(r < pieces)(body)

    barrier = pltpu.get_barrier_semaphore()
    each(n_col - 1, lambda d: pl.semaphore_signal(
        barrier, inc=1, device_id={"col": col_at(d + 1)}, device_id_type=MESH))
    each(n_row - 1, lambda d: pl.semaphore_signal(
        barrier, inc=1, device_id={"row": row_at(d + 1)}, device_id_type=MESH))
    index_pairs = ((rows_in, rows_v, rows_ref), (cols_in, cols_v, cols_ref), (count_in, count_v, count_ref))
    fetches = [
        pltpu.make_async_copy(source, target, in_s.at[k])
        for k, (source, target) in enumerate((
            (cot_ref, cot_all.at[out_id]), (feat_in, feat_ref), (tiles_in, tiles_all.at[in_id]),
            (rows_in, rows_v.at[in_id]), (cols_in, cols_v.at[in_id]), (count_in, count_v.at[in_id]),
            (w_in, w_ref),
        ))
    ]
    for fetch in fetches:
        fetch.start()
    own = place(in_id, col)
    fetches[1].wait()
    feat_all[own] = feat_ref[...].astype(BF16)
    fetches[0].wait()
    pl.semaphore_wait(barrier, n_col + n_row - 2)

    def chain(o, step, sems, d):
        send(cot_all.at[o], cot_all.at[o], sems.at[d], cot_r.at[o], {"row": (out_id + step) * inner + in_id})

    if outer > 1:
        pl.when(out_id < outer - 1)(lambda: chain(out_id, 1, up_s, 0))
        pl.when(out_id > 0)(lambda: chain(out_id, -1, down_s, 0))

    def swap(d):
        to = {"row": out_id * inner + in_at(d + 1)}
        send(feat_all.at[own], feat_all.at[own], y_s.at[0, d], feat_r.at[own], to)
        for k, (source, landing, _) in enumerate(index_pairs):
            send(source, landing.at[in_id], y_s.at[k + 1, d], y_r.at[k, in_id], to)
        send(tiles_in, tiles_all.at[in_id], y_s.at[4, d], y_r.at[3, in_id], to)

    each(inner - 1, swap)

    def feat_out(j, e):
        at = place(j, col)
        each(wide - 1, lambda d: send(
            feat_all.at[at], feat_all.at[at], fx_s.at[e, d], feat_r.at[at], {"col": outer_col(d + 1)}))
        each(near - 1, lambda d: send(
            feat_all.at[at], feat_all.at[at], fn_s.at[e, d], feat_r.at[at], {"col": near_col(d + 1)}))

    feat_out(in_id, 0)
    fetches[6].wait()
    weight = w_ref[...]
    w_hi[...] = weight.astype(BF16)
    w_lo[...] = (weight - w_hi[...].astype(F32)).astype(BF16)

    def pass_on(d):
        def from_below():
            o = out_id - d
            landed(cot_all.at[o], cot_r.at[o])
            pl.when(out_id < outer - 1)(lambda: chain(o, 1, up_s, d))

        def from_above():
            o = out_id + d
            landed(cot_all.at[o], cot_r.at[o])
            pl.when(out_id > 0)(lambda: chain(o, -1, down_s, d))

        pl.when(out_id - d >= 0)(from_below)
        pl.when(out_id + d < outer)(from_above)

    def feat_near(j, e):
        def one(d):
            at = place(j, outer_col(d + 1))
            landed(feat_all.at[at], feat_r.at[at])
            each(near - 1, lambda f: send(
                feat_all.at[at], feat_all.at[at], ff_s.at[e, d, f], feat_r.at[at], {"col": near_col(f + 1)}))
        each(wide - 1, one)

    def feat_in_on(e):
        j = in_at(e + 1)
        landed(feat_all.at[place(j, col)], feat_r.at[place(j, col)])
        feat_out(j, e + 1)

    each(inner - 1, feat_in_on)
    if outer > 1:
        pass_on(1)
    feat_near(in_id, 0)

    for fetch in fetches[2:6]:
        fetch.wait()

    def tiles_landed(e):
        j = in_at(e + 1)
        for k, (_, landing, _) in enumerate(index_pairs):
            landed(landing.at[j], y_r.at[k, j])
        landed(tiles_all.at[j], y_r.at[3, j])

    each(inner - 1, tiles_landed)
    moves = [pltpu.make_async_copy(landing, ref, move_s.at[k]) for k, (_, landing, ref) in enumerate(index_pairs)]
    for move in moves:
        move.start()

    def pad_one(t):
        for j in range(inner):
            one = tiles_all[j, t]
            pad[j, t] = one
            pad_t[j, t] = one.T

    each(slots, pad_one)
    for j in range(inner):
        pad[j, slots] = jnp.zeros((tile, tile), BF16)
        pad_t[j, slots] = jnp.zeros((tile, tile), BF16)
    for move in moves:
        move.wait()
    places = [
        [jnp.where(t < count_ref[j, 0, 0], rows_ref[j, 0, 0, t] * src_tiles + cols_ref[j, 0, 0, t], -1)
         for t in range(slots)] for j in range(inner)
    ]

    def lay(o):
        at = o * tile if isinstance(o, int) else pl.multiple_of(o * tile, tile)
        for j in range(inner):
            for k in range(src_tiles):
                index = jnp.int32(slots)
                for t in range(slots):
                    index = jnp.where(places[j][t] == (o * inner + in_id) * src_tiles + k, t, index)
                p = place(j, k)
                a_ref[pl.ds(at, tile), p * tile:(p + 1) * tile] = pad[j, index]
                at_ref[p * tile:(p + 1) * tile, pl.ds(at, tile)] = pad_t[j, index]

    each(outer, lay)
    each(min(outer - 2, 1), lambda d: pass_on(2))

    def near_landed(j, d):
        def one(e):
            c = lax.rem(wide_id + d, wide) * near + lax.rem(near_id + e + 1, near)
            landed(feat_all.at[place(j, c)], feat_r.at[place(j, c)])
        each(near - 1, one)

    def project(j):
        def one(c, _):
            p = place(j, c)
            block = feat_all[p]
            proj[pl.ds(pl.multiple_of(p * rows_dev, rows_dev), rows_dev), :] = (
                matmul(block, w_hi[...]) + matmul(block, w_lo[...])
            ).astype(BF16)
        lax.fori_loop(0, n_col, one, None)

    def turn(j):
        def one(c, _):
            p = place(j, c)
            feat_t[:, pl.ds(pl.multiple_of(p * rows_dev, rows_dev), rows_dev)] = feat_all[p].T
        lax.fori_loop(0, n_col, one, None)

    each(wide, lambda d: near_landed(in_id, d))
    turn(in_id)
    project(in_id)
    each(inner - 1, lambda e: feat_near(in_at(e + 1), e + 1))
    for e in range(1, inner):
        each(wide, lambda d: near_landed(in_at(e), d))
        turn(in_at(e))

    for e in range(1, inner):
        project(in_at(e))

    each(outer - 3, lambda d: pass_on(d + 3))

    def forward(d):
        o = out_at(d + 1)
        part_send[o] = matmul(
            a_ref[pl.ds(pl.multiple_of(o * tile, tile), tile), :], proj[...]
        ).astype(BF16)
        send(part_send.at[o], z_in.at[out_id], pz_s.at[d], pz_r.at[out_id], {"row": o * inner + in_id})

    each(outer - 1, forward)
    part[...] = matmul(a_ref[pl.ds(pl.multiple_of(out_id * tile, tile), tile), :], proj[...])

    ax_t[...] = matmul(feat_t[...], at_ref[...]).astype(BF16)
    g_part[...] = matmul(
        ax_t[...], cot_all[...].reshape(outer * rows_dev, width)
    ).astype(BF16).reshape(n_col, g_rows, width)

    def g1_out(d):
        c = col_at(d + 1)
        send(g_part.at[c], g1_in.at[col], g1_s.at[d], g1_r.at[col], {"col": c})

    each(n_col - 1, g1_out)

    back[...] = matmul(at_ref[...], cot_all[...].reshape(outer * rows_dev, width)).reshape(back.shape)
    back_send[...] = back[...].astype(BF16)

    def n1_out(d):
        e = lax.rem(near_id + d + 1, near)
        send(back_send.at[e], n1_in.at[near_id], n1_s.at[d], n1_r.at[near_id], {"col": near_col(d + 1)})

    each(near - 1, n1_out)

    def n1_add(d):
        e = lax.rem(near_id + d + 1, near)
        landed(n1_in.at[e], n1_r.at[e])
        back[near_id] += n1_in[e].astype(F32)

    each(near - 1, n1_add)
    n1_sum[...] = back[near_id].astype(BF16)

    def n2_out(d):
        j = in_at(d + 1)
        send(n1_sum.at[j], n2_in.at[in_id], n2_s.at[d], n2_r.at[in_id], {"row": out_id * inner + j})

    each(inner - 1, n2_out)

    gw_part = g_part[col].astype(F32)
    def g1_add(d, total):
        c = col_at(d + 1)
        landed(g1_in.at[c], g1_r.at[c])
        return total + g1_in[c].astype(F32)
    for d in range(n_col - 1):
        gw_part = g1_add(d, gw_part)
    g1_sum[...] = gw_part.astype(BF16).reshape(pieces, g_piece, width)

    def g2_out(d):
        r = row_at(d + 1)
        reducer(r, lambda: send(g1_sum.at[r], g2_in.at[row], g2_s.at[d], g2_r.at[row], {"row": r}))

    each(n_row - 1, g2_out)

    def n2_add(d):
        j = in_at(d + 1)
        landed(n2_in.at[j], n2_r.at[j])
        back[near_id, in_id] += n2_in[j].astype(F32)

    each(inner - 1, n2_add)
    n2_sum[...] = back[near_id, in_id].astype(BF16)

    def n3_out(d):
        w = lax.rem(wide_id + d + 1, wide)
        send(n2_sum.at[w], n3_in.at[wide_id], n3_s.at[d], n3_r.at[wide_id], {"col": outer_col(d + 1)})

    each(wide - 1, n3_out)

    def g2_sum():
        def g2_wait(d):
            r = row_at(d + 1)
            landed(g2_in.at[r], g2_r.at[r])
        each(n_row - 1, g2_wait)
        g2_in[row] = g1_sum[row]
        total = g2_in[0].astype(F32)
        for r in range(1, n_row):
            total = total + g2_in[r].astype(F32)
        gw_all[col, row] = total.astype(BF16)

        def g3_out(d):
            send(gw_all.at[col, row], gw_all.at[col, row], g3_s.at[d], g3_r.at[row], {"row": row_at(d + 1)})
        each(n_row - 1, g3_out)

    reducer(row, g2_sum)

    def to_near(c, r, d):
        def one(e):
            send(gw_all.at[c, r], gw_all.at[c, r], g5_s.at[d, r, e], g4_r.at[c, r], {"col": near_col(e + 1)})
        each(near - 1, one)

    def piece_out(r):
        def one(d):
            send(gw_all.at[col, r], gw_all.at[col, r], g4_s.at[d, r], g4_r.at[col, r], {"col": outer_col(d + 1)})
        each(n_col // near - 1, one)
        to_near(col, r, 0)

    def g3_wait(d):
        r = row_at(d + 1)

        def piece():
            landed(gw_all.at[col, r], g3_r.at[r])
            piece_out(r)
        reducer(r, piece)

    reducer(row, lambda: piece_out(row))
    each(n_row - 1, g3_wait)

    def n3_add(d):
        w = lax.rem(wide_id + d + 1, wide)
        landed(n3_in.at[w], n3_r.at[w])
        back[near_id, in_id, wide_id] += n3_in[w].astype(F32)

    each(wide - 1, n3_add)
    grad_y = back[near_id, in_id, wide_id]
    grad_y = grad_y.astype(BF16)
    gx_ref[...] = matmul(grad_y, w_hi[...], ((1,), (1,))) + matmul(grad_y, w_lo[...], ((1,), (1,)))

    def pass_piece(d):
        c = outer_col(d + 1)

        def one(e):
            r = row_at(e)

            def piece():
                landed(gw_all.at[c, r], g4_r.at[c, r])
                to_near(c, r, d + 1)
            reducer(r, piece)
        each(n_row, one)

    each(n_col // near - 1, pass_piece)

    def z_wait(d):
        o = out_at(d + 1)
        landed(z_in.at[o], pz_r.at[o])
        part[...] += z_in[o].astype(F32)

    each(outer - 1, z_wait)
    agg_ref[...] = part[...].astype(BF16)

    def last_wait(d):
        def one(e):
            c = near_col(e + 1)
            c = lax.rem(c // near + d, n_col // near) * near + c % near
            each(pieces, lambda r: landed(gw_all.at[c, r], g4_r.at[c, r]))
        each(near - 1, one)

    each(n_col // near, last_wait)
    gw_ref[...] = gw_all[...].reshape(width, width)

    def swap_sent(d):
        sent(feat_all.at[0], y_s.at[0, d])
        for k, (source, _, _) in enumerate(index_pairs):
            sent(source, y_s.at[k + 1, d])
        sent(tiles_in, y_s.at[4, d])

    each(inner - 1, swap_sent)
    for j in range(inner):
        each(wide - 1, lambda d: sent(feat_all.at[0], fx_s.at[j, d]))
        each(near - 1, lambda d: sent(feat_all.at[0], fn_s.at[j, d]))
        each(wide - 1, lambda d: each(near - 1, lambda f: sent(feat_all.at[0], ff_s.at[j, d, f])))

    def chain_sent(d):
        def up():
            sent(cot_ref, up_s.at[d])

        def down():
            sent(cot_ref, down_s.at[d])
        pl.when((out_id - d >= 0) & (out_id < outer - 1))(up)
        pl.when((out_id + d < outer) & (out_id > 0))(down)

    if outer > 1:
        each(outer, chain_sent)
    each(outer - 1, lambda d: sent(z_in.at[0], pz_s.at[d]))
    each(near - 1, lambda d: sent(n1_in.at[0], n1_s.at[d]))
    each(inner - 1, lambda d: sent(n2_in.at[0], n2_s.at[d]))
    each(wide - 1, lambda d: sent(n3_in.at[0], n3_s.at[d]))
    each(n_col - 1, lambda d: sent(g1_in.at[0], g1_s.at[d]))
    each(n_row - 1, lambda d: reducer(row_at(d + 1), lambda: sent(g2_in.at[0], g2_s.at[d])))
    reducer(row, lambda: each(n_row - 1, lambda d: sent(g2_in.at[0], g3_s.at[d])))
    each(pieces, lambda r: each(n_col // near - 1, lambda d: sent(g2_in.at[0], g4_s.at[d, r])))
    each(pieces, lambda r: each(n_col // near, lambda d: each(
        near - 1, lambda e: sent(g2_in.at[0], g5_s.at[d, r, e]))))


def write_kernel(agg_ref, gx_ref, gw_ref, agg_out, gx_out, gw_out, agg, gx, narrow, wide, sems):
    loads = [
        pltpu.make_async_copy(source, target, sems.at[k])
        for k, (source, target) in enumerate(((gw_ref, narrow), (agg_ref, agg), (gx_ref, gx)))
    ]
    stores = [
        pltpu.make_async_copy(source, target, sems.at[3 + k])
        for k, (source, target) in enumerate(((wide, gw_out), (agg, agg_out), (gx, gx_out)))
    ]
    for load in loads:
        load.start()
    for k in (1, 2):
        loads[k].wait()
        stores[k].start()
    loads[0].wait()
    wide[...] = narrow[...].astype(F32)
    for k in (0, 1, 2):
        if k == 0:
            stores[k].start()
        stores[k].wait()


def shards(n_col, n_row, features, weight, tiles, tile_rows, tile_cols, tile_count, cotangent):
    slots, tile = tiles.shape[2], tiles.shape[-1]
    rows_dev, width = features.shape
    inner = 2 if n_row % 2 == 0 else 1
    near = 2 if n_col % 2 == 0 else 1
    outer = n_row // inner
    g_rows = width // n_col
    pieces = min(n_row, g_rows // 16)
    g_piece = g_rows // pieces
    pair, half, wide = inner * n_col * rows_dev, outer * rows_dev, n_col // near
    dma = pltpu.SemaphoreType.DMA
    vmem = pl.BlockSpec(memory_space=pltpu.VMEM)
    hbm = pl.BlockSpec(memory_space=pltpu.HBM)
    anywhere = pl.BlockSpec(memory_space=pl.ANY)
    buffers = [
        (features.shape, F32),
        (weight.shape, F32),
        ((inner, *tiles.shape[2:]), BF16),
        ((inner * n_col, rows_dev, width), BF16),
        ((width, pair), BF16),
        ((width, half), BF16),
        ((outer, rows_dev, width), BF16),
        ((inner, slots + 1, tile, tile), BF16),
        ((inner, slots + 1, tile, tile), BF16),
        ((half, pair), BF16),
        ((pair, half), BF16),
        ((width, width), BF16),
        ((width, width), BF16),
        ((pair, width), BF16),
        ((rows_dev, width), F32),
        ((outer, rows_dev, width), BF16),
        ((outer, rows_dev, width), BF16),
        ((near, inner, wide, rows_dev, width), F32),
        ((near, inner, wide, rows_dev, width), BF16),
        ((near, inner, wide, rows_dev, width), BF16),
        ((inner, wide, rows_dev, width), BF16),
        ((inner, wide, rows_dev, width), BF16),
        ((wide, rows_dev, width), BF16),
        ((wide, rows_dev, width), BF16),
        ((n_col, g_rows, width), BF16),
        ((n_col, g_rows, width), BF16),
        ((pieces, g_piece, width), BF16),
        ((n_row, g_piece, width), BF16),
        ((n_col, pieces, g_piece, width), BF16),
    ]
    held = sum(math.prod(shape) * jnp.dtype(kind).itemsize for shape, kind in buffers)
    limit = max(56 * 2**20, min(held + 12 * 2**20, 63 * 2**20))
    sems = [
        (7,), (3,), (5, inner), (4, inner), (inner, wide), (inner, near), (inner, wide, near),
        (inner * n_col,), (outer,), (outer,), (outer,), (outer,), (outer,),
        (near,), (near,), (inner,), (inner,), (wide,), (wide,), (n_col,), (n_col,), (n_row,), (n_row,),
        (n_row,), (n_row,), (n_col, pieces), (n_col, pieces), (n_col, pieces, near),
    ]
    aggregated, grad_x, grad_w = pl.pallas_call(
        functools.partial(layer_kernel, n_col, n_row, inner, near, pieces),
        out_shape=(
            jax.ShapeDtypeStruct((rows_dev, width), BF16),
            jax.ShapeDtypeStruct((rows_dev, width), F32),
            jax.ShapeDtypeStruct((width, width), BF16),
        ),
        in_specs=[hbm] * 7,
        out_specs=(vmem, vmem, vmem),
        scratch_shapes=[
            kind((inner, *one.shape), jnp.int32)
            for kind in (pltpu.SMEM, pltpu.VMEM) for one in (tile_rows, tile_cols, tile_count)
        ]
        + [pltpu.VMEM(shape, kind) for shape, kind in buffers] + [dma(s) for s in sems],
        compiler_params=pltpu.CompilerParams(
            collective_id=0, has_side_effects=True, vmem_limit_bytes=limit
        ),
        name="layer",
    )(
        tile_rows, tile_cols, tile_count,
        features, weight, tiles[0, 0], cotangent,
    )
    return pl.pallas_call(
        write_kernel,
        out_shape=(
            jax.ShapeDtypeStruct((rows_dev, width), BF16),
            jax.ShapeDtypeStruct((rows_dev, width), F32),
            jax.ShapeDtypeStruct((width, width), F32),
        ),
        in_specs=[anywhere] * 3,
        out_specs=(hbm,) * 3,
        scratch_shapes=[
            pltpu.VMEM((rows_dev, width), BF16), pltpu.VMEM((rows_dev, width), F32),
            pltpu.VMEM((width, width), BF16), pltpu.VMEM((width, width), F32), dma((6,)),
        ],
        compiler_params=pltpu.CompilerParams(vmem_limit_bytes=limit),
        name="write",
    )(aggregated, grad_x, grad_w)


def solution(mesh):
    placed = (
        P(("row", "col"), None),
        P(),
        P("col", "row", None, None, None),
        P("col", "row", None),
        P("col", "row", None),
        P("col", "row"),
        P(("col", "row"), None),
    )
    return jax.shard_map(
        functools.partial(shards, mesh.shape["col"], mesh.shape["row"]),
        mesh=mesh,
        in_specs=placed,
        out_specs=(P(("col", "row"), None), P(("row", "col"), None), P()),
        check_vma=False,
    )
```
